32 devices in a mesh: rows: 8 (over y, x, core), cols: 4 (over z).
Axes of the slice: x: 2, y: 2, z: 4, core: 2. Of those that a mesh axis runs over, the one named last changes fastest.
Arguments:
- panel_t: float32 [256, 16384], P('cols', 'rows'), as said below
- trailing: float32 [16384, 1024], P('rows', 'cols'), may hold values from -6 to 6
- prev_lower_t: float32 [256, 16384], P('cols', 'rows'), may hold values from -6 to 6
- prev_upper: float32 [256, 1024], P(None, 'cols'), may hold values from -0.375 to 0.375
- leaf_picks: int32 [8, 256], P('rows'), may hold values from 0 to 2047, as said below
- merge_picks: int32 [7, 256], replicated, may hold values from 0 to 511, as said below
Outputs:
- lower_t: float32 [256, 16384], P('cols', 'rows')
- upper_left: float32 [256, 256], replicated
- upper_right: float32 [256, 1024], P(None, 'cols')
- updated: float32 [16384, 1024], P('rows', 'cols')
- gram: float32 [256, 256], P('cols')
The draws below stay inside these ranges and needn't reach their ends.
Inputs may be any that keep to these rules, and one draw needn't show every extreme that they name: `leaf_picks`: each row lists 256 different row numbers within the 2048 rows of one index of rows. `merge_picks`: each row lists 256 different positions in a stack of two candidate lists. `panel_t`: the rows of the panel at the pivots form a strictly diagonally dominant block.
All inputs are finite; a program needn't handle non-finite values.
Results may differ from the reference program's by a relative error of at most 0.0003.
Values sent between devices are 32-bit elements; how exact they have to be, the bound alone decides.
A program may use at most 64 MiB of HBM per device.

```python
import math
import jax
import jax.numpy as jnp
from jax import lax

B = 256
ROWS_DEV = 2048
M = 16384
TRAIL = 1024
N_ROWS = 8


def forced_row(key, upper_bound, list_width):
    middle_values = jax.random.permutation(key, upper_bound - 2)[:list_width - 2].astype(jnp.int32) + 1
    end_values = jnp.array([0, upper_bound - 1], dtype=jnp.int32)
    joined = jnp.concatenate([middle_values, end_values])
    return jax.random.permutation(jax.random.fold_in(key, 7), joined)


def pick_table(key, row_count, upper_bound, list_width):
    key_list = jax.random.split(key, row_count)
    drawn_rows = jax.vmap(lambda subkey: jax.random.permutation(subkey, upper_bound)[:list_width].astype(jnp.int32))(key_list)
    return drawn_rows.at[0].set(forced_row(key_list[0], upper_bound, list_width))


def pick_lists(key):
    row_devices = M // ROWS_DEV
    leaves = pick_table(jax.random.fold_in(key, 101), row_devices, ROWS_DEV, B)
    merges = pick_table(jax.random.fold_in(key, 202), row_devices - 1, 2 * B, B)
    return (leaves, merges)


def trace_pivots_drawn(merge_picks, row_devices):
    list_width = merge_picks.shape[1]
    leaf_group = jnp.zeros((list_width,), jnp.int32)
    leaf_slot = jnp.arange(list_width, dtype=jnp.int32)
    levels = row_devices.bit_length() - 1
    for section in reversed(range(levels)):
        offset_rows = row_devices - (row_devices >> section)
        position = merge_picks[offset_rows + leaf_group, leaf_slot].astype(jnp.int32)
        right_side = (position >= list_width).astype(jnp.int32)
        leaf_group = 2 * leaf_group + right_side
        leaf_slot = position - list_width * right_side
    return (leaf_group, leaf_slot)


def draw_leaf_picks(key, part):
    return pick_lists(key)[0]


def draw_merge_picks(key, part):
    return pick_lists(key)[1]


def draw_panel_t(key, part):
    leaves, merges = pick_lists(key)
    row_devices = M // ROWS_DEV
    leaf_group, leaf_slot = trace_pivots_drawn(merges, row_devices)
    pivots = leaf_group * ROWS_DEV + leaves[leaf_group, leaf_slot]
    key_list = jax.random.split(jax.random.fold_in(key, 303), 6)
    position = jnp.arange(M, dtype=jnp.float32) / float(max(M - 1, 1))
    normal_part = jax.random.normal(key_list[0], (B, M), jnp.float32)
    row_ramp = 1.0 + 2.0 * position
    common_scale = 0.7
    block_mean = 0.6
    block_diagonal = 1.15
    spread = jnp.exp(jax.random.uniform(key_list[1], (M,), jnp.float32, 0.0, math.log(10.0)))
    common = jax.random.normal(key_list[2], (M,), jnp.float32) * common_scale
    column = 0.8 + 0.6 * jax.random.normal(key_list[3], (B,), jnp.float32)
    values = 0.08 * (spread * row_ramp)[None, :] * (normal_part + column[:, None] * common[None, :])
    wiggle = jax.random.uniform(key_list[4], (B, B), jnp.float32, -1.0, 1.0)
    pivot_scale = jnp.exp(jax.random.uniform(key_list[5], (B,), jnp.float32, 0.0, math.log(3.0)))
    identity = jnp.eye(B, dtype=jnp.float32)
    block = (block_mean + 0.5 * wiggle) * (1.0 / B) * (1.0 - identity) + block_diagonal * identity
    dominant = (pivot_scale[:, None] * block).T
    return values.at[:, pivots].set(dominant)


def level_of(stream_key, shape, cuts, smallest, high):
    gain = 1.0
    for dim, blocks in cuts:
        heights = jax.random.uniform(jax.random.fold_in(jax.random.fold_in(stream_key, 6), dim), (blocks,), jnp.float32, smallest / len(cuts), high / len(cuts))
        gain = gain * jnp.repeat(jnp.exp(heights), shape[dim] // blocks).reshape((-1,) + (1,) * (len(shape) - 1 - dim))
    return gain


def scatter_about(own_key, shape, scale, reach, pieces=(), kind=jnp.bfloat16):
    values = jax.random.normal(own_key, shape, jnp.float32) * scale
    if len(pieces) > 0:
        values = level_of(own_key, shape, pieces, -0.22, 0.18) * values
    return jnp.clip(values, min=-reach, max=reach).astype(kind)


def setup_inputs(seed: int = 0) -> dict:
    keys = jax.random.split(jax.random.key(seed), 7)
    panel_t = draw_panel_t(jax.random.fold_in(keys[6], 71), 0)
    trailing = scatter_about(keys[1], (M, TRAIL), 1.0, 6.0, ((0, 8), (1, 4)), jnp.float32)
    prev_lower_t = scatter_about(keys[2], (B, M), 1.0, 6.0, ((0, 4), (1, 8)), jnp.float32)
    prev_upper = scatter_about(keys[3], (B, TRAIL), B ** -0.5, 0.375, ((1, 4),), jnp.float32)
    leaf_picks = draw_leaf_picks(jax.random.fold_in(keys[6], 71), 0)
    merge_picks = draw_merge_picks(jax.random.fold_in(keys[6], 71), 0)
    return dict(panel_t=panel_t, trailing=trailing, prev_lower_t=prev_lower_t, prev_upper=prev_upper, leaf_picks=leaf_picks, merge_picks=merge_picks)


full_precision = lax.Precision.HIGHEST

def trace_pivots(merge_picks, row_devices):
    list_width = merge_picks.shape[1]
    leaf_group = jnp.zeros((list_width,), jnp.int32)
    leaf_slot = jnp.arange(list_width, dtype=jnp.int32)
    levels = row_devices.bit_length() - 1
    for section in reversed(range(levels)):
        offset_rows = row_devices - (row_devices >> section)
        position = merge_picks[offset_rows + leaf_group, leaf_slot].astype(jnp.int32)
        right_side = (position >= list_width).astype(jnp.int32)
        leaf_group = 2 * leaf_group + right_side
        leaf_slot = position - list_width * right_side
    return (leaf_group, leaf_slot)

def factor(matrix):
    order = matrix.shape[0]
    if order <= 32:
        reduced = matrix
        for column_index in range(order - 1):
            factors = reduced[column_index + 1:, column_index] / reduced[column_index, column_index]
            reduced = reduced.at[column_index + 1:, column_index + 1:].add(-factors[:, None] * reduced[column_index, column_index + 1:][None, :])
            reduced = reduced.at[column_index + 1:, column_index].set(factors)
        return (jnp.tril(reduced, -1) + jnp.eye(order, dtype=matrix.dtype), jnp.triu(reduced))
    middle_index = order // 2
    lower_head, upper_head = factor(matrix[:middle_index, :middle_index])
    upper_side = jax.scipy.linalg.solve_triangular(lower_head, matrix[:middle_index, middle_index:], lower=True, unit_diagonal=True)
    lower_side = jax.scipy.linalg.solve_triangular(upper_head, matrix[middle_index:, :middle_index].T, trans=1, lower=False).T
    schur_block = matrix[middle_index:, middle_index:] - jnp.dot(lower_side, upper_side, precision=full_precision)
    lower_tail, upper_tail = factor(schur_block)
    zero_upper = jnp.zeros((middle_index, order - middle_index), matrix.dtype)
    zero_lower = jnp.zeros((order - middle_index, middle_index), matrix.dtype)
    lower_full = jnp.concatenate([jnp.concatenate([lower_head, zero_upper], 1), jnp.concatenate([lower_side, lower_tail], 1)], 0)
    upper_full = jnp.concatenate([jnp.concatenate([upper_head, upper_side], 1), jnp.concatenate([zero_lower, upper_tail], 1)], 0)
    return (lower_full, upper_full)

def contract_first(left_side, right_side):
    return lax.dot_general(left_side, right_side, (((0,), (0,)), ((), ())), precision=full_precision)

def reference(panel_t, trailing, prev_lower_t, prev_upper, leaf_picks, merge_picks):
    leaf_group, leaf_slot = trace_pivots(merge_picks, N_ROWS)
    pivots = leaf_group * ROWS_DEV + leaf_picks[leaf_group, leaf_slot].astype(jnp.int32)
    pivot_block = panel_t[:, pivots].T
    lower_left, upper_left = factor(pivot_block)
    inverse = jax.scipy.linalg.solve_triangular(upper_left, jnp.eye(B, dtype=upper_left.dtype), lower=False)
    lower_t = jnp.dot(inverse.T, panel_t, precision=full_precision)
    middle_pivots = trailing[pivots] - contract_first(prev_lower_t[:, pivots], prev_upper)
    upper_right = jax.scipy.linalg.solve_triangular(lower_left, middle_pivots, lower=True, unit_diagonal=True)
    trail_blocks = trailing.reshape(N_ROWS, ROWS_DEV, TRAIL)
    prev_blocks = jnp.moveaxis(prev_lower_t.reshape(B, N_ROWS, ROWS_DEV), 1, 0)
    lower_blocks = jnp.moveaxis(lower_t.reshape(B, N_ROWS, ROWS_DEV), 1, 0)

    def update_block(operands):
        trail_rows, prev_rows, lower_rows = operands
        middle = trail_rows - contract_first(prev_rows, prev_upper)
        return middle - contract_first(lower_rows, upper_right)
    updated = lax.map(update_block, (trail_blocks, prev_blocks, lower_blocks)).reshape(M, TRAIL)
    gram = lax.dot_general(lower_t, lower_t, (((1,), (1,)), ((), ())), precision=full_precision) / M
    return (lower_t, upper_left, upper_right, updated, gram)
```

```python
import jax
import jax.numpy as jnp
from jax import lax
from jax.experimental import pallas as pl
from jax.experimental.pallas import tpu as pltpu
from jax.sharding import PartitionSpec as P

full_precision = lax.Precision.HIGH


def from_partner(shard, axis, apart):
    return lax.ppermute(shard, axis, [(i, i ^ 1 << apart) for i in range(lax.axis_size(axis))])


def trace_pivots(merge_picks, row_devices):
    list_width = merge_picks.shape[1]
    leaf_group = jnp.zeros((list_width,), jnp.int32)
    leaf_slot = jnp.arange(list_width, dtype=jnp.int32)
    levels = row_devices.bit_length() - 1
    for section in reversed(range(levels)):
        offset_rows = row_devices - (row_devices >> section)
        position = merge_picks[offset_rows + leaf_group, leaf_slot]
        right_side = (position >= list_width).astype(jnp.int32)
        leaf_group = 2 * leaf_group + right_side
        leaf_slot = position - list_width * right_side
    return (leaf_group, leaf_slot)


def product(left_side, right_side):
    return jnp.dot(left_side, right_side, precision=full_precision)


BLOCK = 32


def pieces(value):
    first = value.astype(jnp.bfloat16)
    rest = value - first.astype(jnp.float32)
    second = rest.astype(jnp.bfloat16)
    third = (rest - second.astype(jnp.float32)).astype(jnp.bfloat16)
    return first, second, third


def thin_product(left_t, right):
    l0, l1, l2 = pieces(left_t)
    r0, r1, r2 = pieces(right)
    left_stack = jnp.concatenate([l0, l0, l1, l1, l0, l2], 0)
    right_stack = jnp.concatenate([r0, r1, r0, r1, r2, r0], 0)
    return lax.dot_general(
        left_stack, right_stack, (((0,), (0,)), ((), ())), preferred_element_type=jnp.float32
    )


def eliminate(tiles):
    sub = lax.broadcasted_iota(jnp.int32, (8, 128), 0)
    groups = BLOCK // 8
    for k in range(BLOCK - 1):
        home, s = k // 8, k % 8
        for chain in tiles:
            row = [jnp.broadcast_to(t[s : s + 1, :], (8, 128)) for t in chain[home]]
            inverse = 1.0 / row[0]
            for g in range(home, groups):
                if g == home and s == 7:
                    continue
                scaled = chain[g][0] * inverse
                if g == home:
                    scaled = jnp.where(sub > s, scaled, 0.0)
                factor = jnp.broadcast_to(scaled[:, k : k + 1], (8, 128))
                chain[g] = [t - factor * r for t, r in zip(chain[g], row)]
    return tiles


def lu_stage(stage, order, w, x, u_ref, linv_ref, uinvt_ref):
    groups = BLOCK // 8
    start = pl.multiple_of(stage * BLOCK, BLOCK)
    rows = pl.ds(start, BLOCK)
    back = lax.rem(order - start, order)
    spare = order // 128
    lane = lax.broadcasted_iota(jnp.int32, (BLOCK, order), 1)
    sub = lax.broadcasted_iota(jnp.int32, (BLOCK, order), 0)
    eye8 = lax.broadcasted_iota(jnp.int32, (8, 128), 1) - lax.broadcasted_iota(
        jnp.int32, (8, 128), 0
    )
    chains = []
    for ref in (w, x):
        turned = pltpu.roll(ref[rows, :], back, 1)
        chain = []
        for g in range(groups):
            part = [turned[8 * g : 8 * g + 8, 128 * t : 128 * t + 128] for t in range(spare)]
            part.append(jnp.where(eye8 == 8 * g, 1.0, 0.0))
            chain.append(part)
        chains.append(chain)
    chains = eliminate(chains)
    full, joined, diagonal = [], [], []
    for chain in chains:
        main = jnp.concatenate(
            [jnp.concatenate([chain[g][t] for g in range(groups)], 0) for t in range(spare)], 1
        )
        extra = jnp.concatenate([chain[g][spare] for g in range(groups)], 0)
        extra = jnp.concatenate([extra] + [jnp.zeros((BLOCK, 128), jnp.float32)] * (spare - 1), 1)
        pivot = jnp.sum(jnp.where(lane == sub, main, 0.0), 1, keepdims=True)
        mixed = jnp.where(lane < BLOCK, extra, main)
        full.append(pltpu.roll(main, start, 1))
        joined.append(pltpu.roll(mixed, start, 1))
        diagonal.append(pivot)
    u_ref[rows, :] = jnp.where(lane >= sub + start, full[0], 0.0)
    reached = lane < start + BLOCK
    inverse_w = 1.0 / diagonal[0]
    inverse_x = 1.0 / diagonal[1]
    linv_ref[rows, :] = jnp.where(reached, joined[0], 0.0)
    uinvt_ref[rows, :] = jnp.where(reached, joined[1] * inverse_x, 0.0)
    lower = jnp.where(reached, 0.0, full[1] * inverse_x)
    upper = jnp.where(reached, 0.0, full[0] * inverse_w)
    cols = lax.broadcasted_iota(jnp.int32, (order, order), 1)
    inside = (cols >= start) & (cols < start + BLOCK)
    w[...] = jnp.where(inside, 0.0, w[...]) - thin_product(lower, joined[0])
    x[...] = jnp.where(inside, 0.0, x[...]) - thin_product(upper, joined[1])


def lu_kernel(a_ref, at_ref, u_ref, linv_ref, uinvt_ref, w, x):
    order = a_ref.shape[0]
    w[...] = a_ref[...]
    x[...] = at_ref[...]

    @pl.loop(0, order // BLOCK)
    def _(stage):
        lu_stage(stage, order, w, x, u_ref, linv_ref, uinvt_ref)


def factor(block, block_t):
    order = block.shape[0]
    shape = jax.ShapeDtypeStruct((order, order), jnp.float32)
    return pl.pallas_call(
        lu_kernel,
        out_shape=[shape] * 3,
        in_specs=[pl.BlockSpec(memory_space=pltpu.VMEM)] * 2,
        out_specs=[pl.BlockSpec(memory_space=pltpu.VMEM)] * 3,
        scratch_shapes=[pltpu.VMEM((order, order), jnp.float32)] * 2,
        compiler_params=pltpu.CompilerParams(vmem_limit_bytes=32 * 1024 * 1024),
        name="block_factors",
    )(block, block_t)


def contract_first(left_side, right_side):
    return lax.dot_general(
        left_side, right_side, (((0,), (0,)), ((), ())), precision=full_precision
    )


def contract_second(left_side, right_side):
    return lax.dot_general(
        left_side, right_side, (((1,), (1,)), ((), ())), precision=full_precision
    )


def body(panel_t, trailing, prev_lower_t, prev_upper, leaf_picks, merge_picks):
    slab_rows = panel_t.shape[0]
    rows_here = panel_t.shape[1]
    row_devices = lax.axis_size("rows")
    own_row = lax.axis_index("rows")
    own_column = lax.axis_index("cols")
    leaf_group, leaf_slot = trace_pivots(merge_picks, row_devices)
    owner_mask = leaf_group == own_row
    local_rows = jnp.take(leaf_picks[0], leaf_slot)
    middle = trailing
    middle = middle - contract_first(
        lax.all_gather(prev_lower_t, "cols", axis=0, tiled=True), prev_upper
    )
    panel_full = lax.all_gather(panel_t, "cols", axis=0, tiled=True)
    candidates = jnp.take(panel_t, leaf_picks[0], axis=1)
    levels = row_devices.bit_length() - 1
    for section in range(levels):
        partner = from_partner(candidates, "rows", section)
        upper_half = own_row >> section & 1
        stacked = jnp.where(
            upper_half == 0,
            jnp.concatenate([candidates, partner], 1),
            jnp.concatenate([partner, candidates], 1),
        )
        merge_index = row_devices - (row_devices >> section) + (own_row >> section + 1)
        selection = lax.dynamic_index_in_dim(merge_picks, merge_index, 0, keepdims=False)
        candidates = jnp.take(stacked, selection, axis=1)
    block_t = lax.all_gather(candidates, "cols", axis=0, tiled=True)
    upper_left, lower_inverse, inverse_t = factor(block_t.T, block_t)
    chosen_rows = jnp.take(middle, local_rows, axis=0)
    pivot_trailing = lax.psum(jnp.where(owner_mask[:, None], chosen_rows, 0.0), "rows")
    upper_right = product(lower_inverse, pivot_trailing)
    lower_full = product(inverse_t, panel_full)
    lower_tile = lax.dynamic_slice_in_dim(lower_full, own_column * slab_rows, slab_rows, 0)
    updated = middle - contract_first(lower_full, upper_right)
    gram_rows = contract_second(lower_tile, lower_full)
    gram = lax.psum(gram_rows, "rows") / (rows_here * row_devices)
    return (lower_tile, upper_left, upper_right, updated, gram)


def solution(mesh):
    return jax.shard_map(
        body,
        mesh=mesh,
        in_specs=(
            P("cols", "rows"),
            P("rows", "cols"),
            P("cols", "rows"),
            P(None, "cols"),
            P("rows", None),
            P(),
        ),
        out_specs=(P("cols", "rows"), P(), P(None, "cols"), P("rows", "cols"), P("cols", None)),
        check_vma=False,
    )
```

```python
import functools
import jax
import jax.numpy as jnp
from jax import lax
from jax.experimental import pallas as pl
from jax.experimental.pallas import tpu as pltpu
from jax.sharding import PartitionSpec as P

MESH = pl.DeviceIdType.MESH
PIECES = 8

BLOCK = 32


def pieces(value):
    first = value.astype(jnp.bfloat16)
    rest = value - first.astype(jnp.float32)
    second = rest.astype(jnp.bfloat16)
    third = (rest - second.astype(jnp.float32)).astype(jnp.bfloat16)
    return first, second, third


def thin_product(left_t, right):
    l0, l1, l2 = pieces(left_t)
    r0, r1, r2 = pieces(right)
    left_stack = jnp.concatenate([l0, l0, l1, l1, l0, l2], 0)
    right_stack = jnp.concatenate([r0, r1, r0, r1, r2, r0], 0)
    return lax.dot_general(
        left_stack, right_stack, (((0,), (0,)), ((), ())), preferred_element_type=jnp.float32
    )


def eliminate(tiles):
    sub = lax.broadcasted_iota(jnp.int32, (8, 128), 0)
    groups = BLOCK // 8
    for k in range(BLOCK - 1):
        home, s = k // 8, k % 8
        for chain in tiles:
            row = [jnp.broadcast_to(t[s : s + 1, :], (8, 128)) for t in chain[home]]
            inverse = 1.0 / row[0]
            for g in range(home, groups):
                if g == home and s == 7:
                    continue
                scaled = chain[g][0] * inverse
                if g == home:
                    scaled = jnp.where(sub > s, scaled, 0.0)
                factor = jnp.broadcast_to(scaled[:, k : k + 1], (8, 128))
                chain[g] = [t - factor * r for t, r in zip(chain[g], row)]
    return tiles


def lu_stage(stage, order, w, x, u_ref, linv_ref, uinvt_ref):
    groups = BLOCK // 8
    start = pl.multiple_of(stage * BLOCK, BLOCK)
    rows = pl.ds(start, BLOCK)
    back = lax.rem(order - start, order)
    spare = order // 128
    lane = lax.broadcasted_iota(jnp.int32, (BLOCK, order), 1)
    sub = lax.broadcasted_iota(jnp.int32, (BLOCK, order), 0)
    eye8 = lax.broadcasted_iota(jnp.int32, (8, 128), 1) - lax.broadcasted_iota(
        jnp.int32, (8, 128), 0
    )
    chains = []
    for ref in (w, x):
        turned = pltpu.roll(ref[rows, :], back, 1)
        chain = []
        for g in range(groups):
            part = [turned[8 * g : 8 * g + 8, 128 * t : 128 * t + 128] for t in range(spare)]
            part.append(jnp.where(eye8 == 8 * g, 1.0, 0.0))
            chain.append(part)
        chains.append(chain)
    chains = eliminate(chains)
    full, joined, diagonal = [], [], []
    for chain in chains:
        main = jnp.concatenate(
            [jnp.concatenate([chain[g][t] for g in range(groups)], 0) for t in range(spare)], 1
        )
        extra = jnp.concatenate([chain[g][spare] for g in range(groups)], 0)
        extra = jnp.concatenate([extra] + [jnp.zeros((BLOCK, 128), jnp.float32)] * (spare - 1), 1)
        pivot = jnp.sum(jnp.where(lane == sub, main, 0.0), 1, keepdims=True)
        mixed = jnp.where(lane < BLOCK, extra, main)
        full.append(pltpu.roll(main, start, 1))
        joined.append(pltpu.roll(mixed, start, 1))
        diagonal.append(pivot)
    u_ref[rows, :] = jnp.where(lane >= sub + start, full[0], 0.0)
    reached = lane < start + BLOCK
    inverse_w = 1.0 / diagonal[0]
    inverse_x = 1.0 / diagonal[1]
    linv_ref[rows, :] = jnp.where(reached, joined[0], 0.0)
    uinvt_ref[rows, :] = jnp.where(reached, joined[1] * inverse_x, 0.0)
    lower = jnp.where(reached, 0.0, full[1] * inverse_x)
    upper = jnp.where(reached, 0.0, full[0] * inverse_w)
    cols = lax.broadcasted_iota(jnp.int32, (order, order), 1)
    inside = (cols >= start) & (cols < start + BLOCK)
    w[...] = jnp.where(inside, 0.0, w[...]) - thin_product(lower, joined[0])
    x[...] = jnp.where(inside, 0.0, x[...]) - thin_product(upper, joined[1])


def halves(value):
    first = value.astype(jnp.bfloat16)
    return first, (value - first.astype(jnp.float32)).astype(jnp.bfloat16)


def product(left, right, left_dim=1, right_dim=0):
    dims = (((left_dim,), (right_dim,)), ((), ()))
    a0, a1 = halves(left)
    b0, b1 = halves(right)
    dot = functools.partial(
        lax.dot_general, dimension_numbers=dims, preferred_element_type=jnp.float32
    )
    return dot(a0, b0) + (dot(a0, b1) + dot(a1, b0))


def trace_rows(merge_ref, leaf_ref, row_devices, own_row):
    width = merge_ref.shape[1]
    lane = lax.broadcasted_iota(jnp.int32, (width, width), 1)
    slot = lax.broadcasted_iota(jnp.int32, (width, 1), 0)
    group = jnp.zeros((width, 1), jnp.int32)

    def look_up(table):
        found = jnp.where(lane == slot, table.astype(jnp.float32), 0.0)
        return jnp.sum(found, 1, keepdims=True).astype(jnp.int32)

    for section in reversed(range(row_devices.bit_length() - 1)):
        offset = row_devices - (row_devices >> section)
        table = jnp.broadcast_to(merge_ref[offset : offset + 1, :], (width, width))
        for g in range(1, row_devices >> (section + 1)):
            line = merge_ref[offset + g : offset + g + 1, :]
            table = jnp.where(group == g, line, table)
        position = look_up(table)
        right_side = (position >= width).astype(jnp.int32)
        group = 2 * group + right_side
        slot = position - width * right_side
    local = look_up(jnp.broadcast_to(leaf_ref[...], (width, width)))
    return jnp.where(group == own_row, local, -1)


def step_kernel(
    row_devices,
    col_devices,
    panel_ref,
    trailing_ref,
    prev_ref,
    prev_upper_ref,
    leaf_ref,
    merge_ref,
    lower_ref,
    u_ref,
    right_ref,
    updated_ref,
    gram_ref,
    tall,
    picked,
    picked_in,
    block,
    trail,
    trail_in,
    trail_all,
    w,
    x,
    linv,
    uinvt,
    lower_full,
    gram_in,
    tall_send,
    tall_recv,
    row_send,
    row_recv,
    zone_send,
    zone_recv,
):
    slab, rows_here = panel_ref.shape
    order = merge_ref.shape[1]
    trail_cols = trailing_ref.shape[1]
    share = order // row_devices
    span = rows_here // PIECES
    own_row = lax.axis_index("rows")
    own_col = lax.axis_index("cols")

    barrier = pltpu.get_barrier_semaphore()

    @pl.loop(1, row_devices)
    def _(d):
        pl.semaphore_signal(
            barrier,
            inc=1,
            device_id={"rows": lax.rem(own_row + d, row_devices)},
            device_id_type=MESH,
        )

    @pl.loop(1, col_devices)
    def _(d):
        pl.semaphore_signal(
            barrier,
            inc=1,
            device_id={"cols": lax.rem(own_col + d, col_devices)},
            device_id_type=MESH,
        )

    for q in range(PIECES):
        part = slice(q * span, (q + 1) * span)
        tall[q, own_col, :slab, :] = panel_ref[:, part]
        tall[q, own_col, slab:, :] = prev_ref[:, part]

    pl.semaphore_wait(barrier, row_devices + col_devices - 2)

    def tall_copy(q, source, way, to):
        place = tall.at[q, source]
        return pltpu.make_async_remote_copy(
            src_ref=place,
            dst_ref=place,
            send_sem=tall_send.at[way, source, q],
            recv_sem=tall_recv.at[source, q],
            device_id={"cols": to},
            device_id_type=MESH,
        )

    def tick(time):
        @pl.loop(0, col_devices)
        def _(hop):
            q = time - hop

            @pl.when((q >= 0) & (q < PIECES))
            def _():
                up = own_col - hop
                down = own_col + hop

                @pl.when((hop > 0) & (up >= 0))
                def _():
                    tall_copy(q, up, 0, own_col - 1).wait_recv()

                @pl.when((up >= 0) & (own_col < col_devices - 1))
                def _():
                    tall_copy(q, up, 0, own_col + 1).start()

                @pl.when((hop > 0) & (down < col_devices))
                def _():
                    tall_copy(q, down, 1, own_col + 1).wait_recv()

                @pl.when((down < col_devices) & (own_col > 0))
                def _():
                    tall_copy(q, down, 1, own_col - 1).start()

    def share_of(d):
        return pl.ds(pl.multiple_of(lax.rem(own_row + d, row_devices) * share, share), share)

    def row_copy(kind, d, src, dst):
        return pltpu.make_async_remote_copy(
            src_ref=src,
            dst_ref=dst,
            send_sem=row_send.at[kind, d],
            recv_sem=row_recv.at[kind, d],
            device_id={"rows": lax.rem(own_row + d, row_devices)},
            device_id_type=MESH,
        )

    def picked_copy(d):
        return row_copy(0, d, picked.at[share_of(d), :], picked_in.at[d])

    def block_copy(d):
        return row_copy(1, d, block.at[own_row], block.at[own_row])

    def trail_copy(d):
        return row_copy(2, d, trail.at[share_of(d), :], trail_in.at[d])

    def trail_out_copy(d):
        return row_copy(3, d, trail_all.at[own_row], trail_all.at[own_row])

    def gram_copy(d):
        return row_copy(4, d, gram_in.at[0], gram_in.at[d])

    def zone_copy(d):
        return pltpu.make_async_remote_copy(
            src_ref=block.at[own_row, own_col],
            dst_ref=block.at[own_row, own_col],
            send_sem=zone_send.at[d],
            recv_sem=zone_recv.at[d],
            device_id={"cols": lax.rem(own_col + d, col_devices)},
            device_id_type=MESH,
        )

    def start_all(copy, count):
        @pl.loop(1, count)
        def _(d):
            copy(d).start()

    def land_all(copy, count):
        @pl.loop(1, count)
        def _(d):
            copy(d).wait_recv()

    def sent_all(copy, count):
        @pl.loop(1, count)
        def _(d):
            copy(d).wait_send()

    target = trace_rows(merge_ref, leaf_ref, row_devices, own_row)
    lane = lax.broadcasted_iota(jnp.int32, (order, span), 1)

    def one_hot(q):
        return jnp.where(lane + q * span == target, 1.0, 0.0).astype(jnp.bfloat16)

    total = jnp.zeros((order, 128), jnp.float32)
    for q in range(PIECES):
        stack = tall[q, own_col]
        if 2 * slab < 128:
            stack = jnp.concatenate([stack, jnp.zeros((128 - 2 * slab, span), jnp.float32)], 0)
        found = lax.dot_general(
            one_hot(q),
            jnp.concatenate(pieces(stack), 0),
            (((1,), (1,)), ((), ())),
            preferred_element_type=jnp.float32,
        )
        total = total + (found[:, :128] + found[:, 128:256] + found[:, 256:])
    picked[...] = total
    start_all(picked_copy, row_devices)
    tick(0)

    total = jnp.zeros((order, trail_cols), jnp.float32)
    for q in range(PIECES):
        chosen = one_hot(q)
        for part in pieces(trailing_ref[q * span : (q + 1) * span, :]):
            total = total + jnp.dot(chosen, part, preferred_element_type=jnp.float32)
    trail[...] = total

    land_all(picked_copy, row_devices)
    total = picked[share_of(0), :]
    for d in range(1, row_devices):
        total = total + picked_in[d]
    block[own_row, own_col] = total
    start_all(zone_copy, col_devices)
    land_all(zone_copy, col_devices)
    start_all(block_copy, row_devices)
    start_all(trail_copy, row_devices)
    land_all(block_copy, row_devices)
    tick(1)

    def gathered(first):
        parts = []
        for z in range(col_devices):
            parts.append(block[:, z].reshape(order, 128)[:, first : first + slab])
        return jnp.concatenate(parts, 1)

    matrix = gathered(0)
    w[...] = matrix
    x[...] = matrix.T

    def stages(first, last):
        @pl.loop(first, last)
        def _(stage):
            lu_stage(stage, order, w, x, u_ref, linv, uinvt)

    count = order // BLOCK
    stages(0, count // 4)
    land_all(trail_copy, row_devices)
    total = trail[share_of(0), :]
    for d in range(1, row_devices):
        total = total + trail_in[d]
    trail_all[own_row] = total
    start_all(trail_out_copy, row_devices)
    tick(2)
    stages(count // 4, 5 * count // 8)
    tick(3)
    stages(5 * count // 8, count)

    @pl.loop(4, col_devices + 1)
    def _(time):
        tick(time)

    land_all(trail_out_copy, row_devices)
    chosen = trail_all[...].reshape(order, trail_cols)
    chosen = chosen - product(gathered(slab), prev_upper_ref[...])
    right_ref[...] = product(linv[...], chosen)
    gram_in[0] = jnp.zeros((slab, order), jnp.float32)

    @pl.loop(0, PIECES)
    def _(q):
        here = pl.ds(pl.multiple_of(q * span, span), span)
        panel_full = tall[q, :, :slab, :].reshape(order, span)
        prev_full = tall[q, :, slab:, :].reshape(order, span)
        lower = product(uinvt[...], panel_full)
        lower_full[...] = lower
        tile = lower_full[pl.ds(pl.multiple_of(own_col * slab, slab), slab), :]
        lower_ref[:, here] = tile
        gram_in[0] += product(tile, lower, 1, 1)
        middle = trailing_ref[here, :] - product(prev_full, prev_upper_ref[...], 0, 0)
        updated_ref[here, :] = middle - product(lower, right_ref[...], 0, 0)
        tick(q + col_devices + 1)

    start_all(gram_copy, row_devices)
    sent_all(picked_copy, row_devices)
    sent_all(zone_copy, col_devices)
    sent_all(block_copy, row_devices)
    sent_all(trail_copy, row_devices)
    sent_all(trail_out_copy, row_devices)

    @pl.loop(0, PIECES)
    def _(q):
        @pl.loop(0, col_devices)
        def _(source):
            @pl.when((source <= own_col) & (own_col < col_devices - 1))
            def _():
                tall_copy(q, source, 0, own_col + 1).wait_send()

            @pl.when((source >= own_col) & (own_col > 0))
            def _():
                tall_copy(q, source, 1, own_col - 1).wait_send()

    land_all(gram_copy, row_devices)
    total = gram_in[0]
    for d in range(1, row_devices):
        total = total + gram_in[d]
    gram_ref[...] = total / (rows_here * row_devices)
    sent_all(gram_copy, row_devices)


def body(row_devices, col_devices, panel_t, trailing, prev_lower_t, prev_upper, leaf, merge):
    slab, rows_here = panel_t.shape
    order = merge.shape[1]
    trail_cols = trailing.shape[1]
    share = order // row_devices
    span = rows_here // PIECES
    real = jnp.float32
    square = pltpu.VMEM((order, order), real)
    vmem = pl.BlockSpec(memory_space=pltpu.VMEM)
    dma = pltpu.SemaphoreType.DMA
    return pl.pallas_call(
        functools.partial(step_kernel, row_devices, col_devices),
        out_shape=[
            jax.ShapeDtypeStruct((slab, rows_here), real),
            jax.ShapeDtypeStruct((order, order), real),
            jax.ShapeDtypeStruct((order, trail_cols), real),
            jax.ShapeDtypeStruct((rows_here, trail_cols), real),
            jax.ShapeDtypeStruct((slab, order), real),
        ],
        in_specs=[vmem] * 6,
        out_specs=[vmem] * 5,
        scratch_shapes=[
            pltpu.VMEM((PIECES, col_devices, 2 * slab, span), real),
            pltpu.VMEM((order, 128), real),
            pltpu.VMEM((row_devices, share, 128), real),
            pltpu.VMEM((row_devices, col_devices, share, 128), real),
            pltpu.VMEM((order, trail_cols), real),
            pltpu.VMEM((row_devices, share, trail_cols), real),
            pltpu.VMEM((row_devices, share, trail_cols), real),
            square,
            square,
            square,
            square,
            pltpu.VMEM((order, span), real),
            pltpu.VMEM((row_devices, slab, order), real),
            dma((2, col_devices, PIECES)),
            dma((col_devices, PIECES)),
            dma((5, row_devices)),
            dma((5, row_devices)),
            dma((col_devices,)),
            dma((col_devices,)),
        ],
        compiler_params=pltpu.CompilerParams(
            collective_id=0, has_side_effects=True, vmem_limit_bytes=48 * 1024 * 1024
        ),
        name="panel_step",
    )(panel_t, trailing, prev_lower_t, prev_upper, leaf, merge)


def solution(mesh):
    return jax.shard_map(
        functools.partial(body, mesh.shape["rows"], mesh.shape["cols"]),
        mesh=mesh,
        in_specs=(
            P("cols", "rows"),
            P("rows", "cols"),
            P("cols", "rows"),
            P(None, "cols"),
            P("rows", None),
            P(),
        ),
        out_specs=(P("cols", "rows"), P(), P(None, "cols"), P("rows", "cols"), P("cols", None)),
        check_vma=False,
    )
```

```python
import functools
import jax
import jax.numpy as jnp
from jax import lax
from jax.experimental import pallas as pl
from jax.experimental.pallas import tpu as pltpu
from jax.sharding import PartitionSpec as P

MESH = pl.DeviceIdType.MESH
PIECES = 8

BLOCK = 32


def pieces(value):
    first = value.astype(jnp.bfloat16)
    rest = value - first.astype(jnp.float32)
    second = rest.astype(jnp.bfloat16)
    third = (rest - second.astype(jnp.float32)).astype(jnp.bfloat16)
    return first, second, third


def thin_product(left_t, right):
    l0, l1, l2 = pieces(left_t)
    r0, r1, r2 = pieces(right)
    left_stack = jnp.concatenate([l0, l0, l1, l1, l0, l2], 0)
    right_stack = jnp.concatenate([r0, r1, r0, r1, r2, r0], 0)
    return lax.dot_general(
        left_stack, right_stack, (((0,), (0,)), ((), ())), preferred_element_type=jnp.float32
    )


def eliminate(tiles):
    sub = lax.broadcasted_iota(jnp.int32, (8, 128), 0)
    groups = BLOCK // 8
    for k in range(BLOCK - 1):
        home, s = k // 8, k % 8
        for chain in tiles:
            row = [jnp.broadcast_to(t[s : s + 1, :], (8, 128)) for t in chain[home]]
            inverse = 1.0 / row[0]
            for g in range(home, groups):
                if g == home and s == 7:
                    continue
                scaled = chain[g][0] * inverse
                if g == home:
                    scaled = jnp.where(sub > s, scaled, 0.0)
                factor = jnp.broadcast_to(scaled[:, k : k + 1], (8, 128))
                chain[g] = [t - factor * r for t, r in zip(chain[g], row)]
    return tiles


def lu_stage(stage, order, w, x, u_ref, linv_ref, uinvt_ref):
    groups = BLOCK // 8
    start = pl.multiple_of(stage * BLOCK, BLOCK)
    rows = pl.ds(start, BLOCK)
    back = lax.rem(order - start, order)
    spare = order // 128
    lane = lax.broadcasted_iota(jnp.int32, (BLOCK, order), 1)
    sub = lax.broadcasted_iota(jnp.int32, (BLOCK, order), 0)
    eye8 = lax.broadcasted_iota(jnp.int32, (8, 128), 1) - lax.broadcasted_iota(
        jnp.int32, (8, 128), 0
    )
    chains = []
    for ref in (w, x):
        turned = pltpu.roll(ref[rows, :], back, 1)
        chain = []
        for g in range(groups):
            part = [turned[8 * g : 8 * g + 8, 128 * t : 128 * t + 128] for t in range(spare)]
            part.append(jnp.where(eye8 == 8 * g, 1.0, 0.0))
            chain.append(part)
        chains.append(chain)
    chains = eliminate(chains)
    full, joined, diagonal = [], [], []
    for chain in chains:
        main = jnp.concatenate(
            [jnp.concatenate([chain[g][t] for g in range(groups)], 0) for t in range(spare)], 1
        )
        extra = jnp.concatenate([chain[g][spare] for g in range(groups)], 0)
        extra = jnp.concatenate([extra] + [jnp.zeros((BLOCK, 128), jnp.float32)] * (spare - 1), 1)
        pivot = jnp.sum(jnp.where(lane == sub, main, 0.0), 1, keepdims=True)
        mixed = jnp.where(lane < BLOCK, extra, main)
        full.append(pltpu.roll(main, start, 1))
        joined.append(pltpu.roll(mixed, start, 1))
        diagonal.append(pivot)
    u_ref[rows, :] = jnp.where(lane >= sub + start, full[0], 0.0)
    reached = lane < start + BLOCK
    inverse_w = 1.0 / diagonal[0]
    inverse_x = 1.0 / diagonal[1]
    linv_ref[rows, :] = jnp.where(reached, joined[0], 0.0)
    uinvt_ref[rows, :] = jnp.where(reached, joined[1] * inverse_x, 0.0)
    lower = jnp.where(reached, 0.0, full[1] * inverse_x)
    upper = jnp.where(reached, 0.0, full[0] * inverse_w)
    cols = lax.broadcasted_iota(jnp.int32, (order, order), 1)
    inside = (cols >= start) & (cols < start + BLOCK)
    w[...] = jnp.where(inside, 0.0, w[...]) - thin_product(lower, joined[0])
    x[...] = jnp.where(inside, 0.0, x[...]) - thin_product(upper, joined[1])


def halves(value):
    first = value.astype(jnp.bfloat16)
    return first, (value - first.astype(jnp.float32)).astype(jnp.bfloat16)


def product(left, right, left_dim=1, right_dim=0):
    dims = (((left_dim,), (right_dim,)), ((), ()))
    a0, a1 = halves(left)
    b0, b1 = halves(right)
    dot = functools.partial(
        lax.dot_general, dimension_numbers=dims, preferred_element_type=jnp.float32
    )
    return dot(a0, b0) + (dot(a0, b1) + dot(a1, b0))


def trace_rows(merge_ref, leaf_ref, row_devices, own_row):
    width = merge_ref.shape[1]
    lane = lax.broadcasted_iota(jnp.int32, (width, width), 1)
    slot = lax.broadcasted_iota(jnp.int32, (width, 1), 0)
    group = jnp.zeros((width, 1), jnp.int32)

    def look_up(table):
        found = jnp.where(lane == slot, table.astype(jnp.float32), 0.0)
        return jnp.sum(found, 1, keepdims=True).astype(jnp.int32)

    for section in reversed(range(row_devices.bit_length() - 1)):
        offset = row_devices - (row_devices >> section)
        table = jnp.broadcast_to(merge_ref[offset : offset + 1, :], (width, width))
        for g in range(1, row_devices >> (section + 1)):
            line = merge_ref[offset + g : offset + g + 1, :]
            table = jnp.where(group == g, line, table)
        position = look_up(table)
        right_side = (position >= width).astype(jnp.int32)
        group = 2 * group + right_side
        slot = position - width * right_side
    local = look_up(jnp.broadcast_to(leaf_ref[...], (width, width)))
    return jnp.where(group == own_row, local, -1)


def step_kernel(
    row_devices,
    col_devices,
    panel_hbm,
    trailing_hbm,
    prev_hbm,
    prev_upper_hbm,
    leaf_hbm,
    merge_hbm,
    lower_hbm,
    u_hbm,
    right_hbm,
    updated_hbm,
    gram_hbm,
    trailing_ref,
    prev_upper_ref,
    leaf_ref,
    merge_ref,
    lower_ref,
    u_ref,
    right_ref,
    gram_ref,
    tall,
    picked,
    picked_in,
    block,
    trail,
    trail_in,
    trail_all,
    w,
    x,
    linv,
    uinvt,
    lower_full,
    gram_in,
    tall_send,
    tall_recv,
    row_send,
    row_recv,
    zone_send,
    zone_recv,
    own_sem,
    in_sem,
    piece_sem,
    out_sem,
):
    slab, rows_here = panel_hbm.shape
    order = merge_ref.shape[1]
    trail_cols = trailing_ref.shape[1]
    share = order // row_devices
    span = rows_here // PIECES
    own_row = lax.axis_index("rows")
    own_col = lax.axis_index("cols")

    barrier = pltpu.get_barrier_semaphore()

    @pl.loop(1, row_devices)
    def _(d):
        pl.semaphore_signal(
            barrier,
            inc=1,
            device_id={"rows": lax.rem(own_row + d, row_devices)},
            device_id_type=MESH,
        )

    @pl.loop(1, col_devices)
    def _(d):
        pl.semaphore_signal(
            barrier,
            inc=1,
            device_id={"cols": lax.rem(own_col + d, col_devices)},
            device_id_type=MESH,
        )

    own_copies = []
    for q in range(PIECES):
        part = pl.ds(q * span, span)
        for kind, (source, rows) in enumerate(
            ((panel_hbm, pl.ds(0, slab)), (prev_hbm, pl.ds(slab, slab)))
        ):
            own_copies.append(
                pltpu.make_async_copy(
                    source.at[:, part], tall.at[q, own_col, rows, :], own_sem.at[kind, q]
                )
            )
    loads = [
        pltpu.make_async_copy(source, place, in_sem.at[i])
        for i, (source, place) in enumerate(
            (
                (merge_hbm, merge_ref),
                (leaf_hbm, leaf_ref),
                (trailing_hbm, trailing_ref),
                (prev_upper_hbm, prev_upper_ref),
            )
        )
    ]
    for copy in loads[:2] + own_copies + loads[2:]:
        copy.start()
    for copy in own_copies:
        copy.wait()
    pl.semaphore_wait(barrier, row_devices + col_devices - 2)

    def tall_copy(q, source, way, to):
        place = tall.at[q, source]
        return pltpu.make_async_remote_copy(
            src_ref=place,
            dst_ref=place,
            send_sem=tall_send.at[way, source, q],
            recv_sem=tall_recv.at[source, q],
            device_id={"cols": to},
            device_id_type=MESH,
        )

    def step(hop, q):
        up = own_col - hop
        down = own_col + hop
        if hop > 0:

            @pl.when(up >= 0)
            def _():
                tall_copy(q, up, 0, own_col - 1).wait_recv()

        @pl.when((up >= 0) & (own_col < col_devices - 1))
        def _():
            tall_copy(q, up, 0, own_col + 1).start()

        if hop > 0:

            @pl.when(down < col_devices)
            def _():
                tall_copy(q, down, 1, own_col + 1).wait_recv()

        @pl.when((down < col_devices) & (own_col > 0))
        def _():
            tall_copy(q, down, 1, own_col - 1).start()

    def share_of(d):
        return pl.ds(pl.multiple_of(lax.rem(own_row + d, row_devices) * share, share), share)

    def row_copy(kind, d, src, dst):
        return pltpu.make_async_remote_copy(
            src_ref=src,
            dst_ref=dst,
            send_sem=row_send.at[kind, d],
            recv_sem=row_recv.at[kind, d],
            device_id={"rows": lax.rem(own_row + d, row_devices)},
            device_id_type=MESH,
        )

    def picked_copy(d):
        return row_copy(0, d, picked.at[share_of(d), :], picked_in.at[d])

    def block_copy(d):
        return row_copy(1, d, block.at[own_row], block.at[own_row])

    def trail_copy(d):
        return row_copy(2, d, trail.at[share_of(d), :], trail_in.at[d])

    def trail_out_copy(d):
        return row_copy(3, d, trail_all.at[own_row], trail_all.at[own_row])

    def gram_copy(d):
        return row_copy(4, d, gram_in.at[0], gram_in.at[d])

    def zone_copy(d):
        return pltpu.make_async_remote_copy(
            src_ref=block.at[own_row, own_col],
            dst_ref=block.at[own_row, own_col],
            send_sem=zone_send.at[d],
            recv_sem=zone_recv.at[d],
            device_id={"cols": lax.rem(own_col + d, col_devices)},
            device_id_type=MESH,
        )

    def start_all(copy, count):
        @pl.loop(1, count)
        def _(d):
            copy(d).start()

    def land_all(copy, count):
        @pl.loop(1, count)
        def _(d):
            copy(d).wait_recv()

    def sent_all(copy, count):
        @pl.loop(1, count)
        def _(d):
            copy(d).wait_send()

    for q in range(2):
        step(0, q)
    loads[0].wait()
    loads[1].wait()
    target = trace_rows(merge_ref, leaf_ref, row_devices, own_row)
    lane = lax.broadcasted_iota(jnp.int32, (order, span), 1)

    def one_hot(q):
        return jnp.where(lane + q * span == target, 1.0, 0.0).astype(jnp.bfloat16)

    total = jnp.zeros((order, 128), jnp.float32)
    for q in range(PIECES):
        stack = tall[q, own_col]
        if 2 * slab < 128:
            stack = jnp.concatenate([stack, jnp.zeros((128 - 2 * slab, span), jnp.float32)], 0)
        found = lax.dot_general(
            one_hot(q),
            jnp.concatenate(pieces(stack), 0),
            (((1,), (1,)), ((), ())),
            preferred_element_type=jnp.float32,
        )
        total = total + (found[:, :128] + found[:, 128:256] + found[:, 256:])
    picked[...] = total
    start_all(picked_copy, row_devices)
    loads[2].wait()
    loads[3].wait()

    total = jnp.zeros((order, trail_cols), jnp.float32)
    for q in range(PIECES):
        chosen = one_hot(q)
        for part in pieces(trailing_ref[q * span : (q + 1) * span, :]):
            total = total + jnp.dot(chosen, part, preferred_element_type=jnp.float32)
    trail[...] = total

    land_all(picked_copy, row_devices)
    total = picked[share_of(0), :]
    for d in range(1, row_devices):
        total = total + picked_in[d]
    block[own_row, own_col] = total
    start_all(zone_copy, col_devices)
    land_all(zone_copy, col_devices)
    start_all(block_copy, row_devices)
    start_all(trail_copy, row_devices)
    for q in range(2, PIECES):
        step(0, q)
    land_all(block_copy, row_devices)

    def gathered(first):
        parts = []
        for z in range(col_devices):
            parts.append(block[:, z].reshape(order, 128)[:, first : first + slab])
        return jnp.concatenate(parts, 1)

    matrix = gathered(0)
    w[...] = matrix
    x[...] = matrix.T

    count = order // BLOCK

    @pl.loop(0, count)
    def _(stage):
        lu_stage(stage, order, w, x, u_ref, linv, uinvt)
        for part in range(PIECES // count):
            step(1, stage * (PIECES // count) + part)

        @pl.when(stage == 2)
        def _():
            land_all(trail_copy, row_devices)
            total = trail[share_of(0), :]
            for d in range(1, row_devices):
                total = total + trail_in[d]
            trail_all[own_row] = total
            start_all(trail_out_copy, row_devices)

    land_all(trail_out_copy, row_devices)
    chosen = trail_all[...].reshape(order, trail_cols)
    chosen = chosen - product(gathered(slab), prev_upper_ref[...])
    right_ref[...] = product(linv[...], chosen)
    gram_in[0] = jnp.zeros((slab, order), jnp.float32)
    u_copy = pltpu.make_async_copy(u_ref, u_hbm, out_sem.at[0])
    right_copy = pltpu.make_async_copy(right_ref, right_hbm, out_sem.at[1])
    u_copy.start()
    right_copy.start()
    for hop in range(2, col_devices - 1):

        @pl.loop(0, PIECES)
        def _(q):
            step(hop, q)

    def piece_copies(q):
        here = pl.ds(pl.multiple_of(q * span, span), span)
        return (
            pltpu.make_async_copy(lower_ref.at[:, here], lower_hbm.at[:, here], piece_sem.at[0, q]),
            pltpu.make_async_copy(
                trailing_ref.at[here, :], updated_hbm.at[here, :], piece_sem.at[1, q]
            ),
        )

    @pl.loop(0, PIECES)
    def _(q):
        step(col_devices - 1, q)
        here = pl.ds(pl.multiple_of(q * span, span), span)
        panel_full = tall[q, :, :slab, :].reshape(order, span)
        prev_full = tall[q, :, slab:, :].reshape(order, span)
        lower = product(uinvt[...], panel_full)
        lower_full[...] = lower
        tile = lower_full[pl.ds(pl.multiple_of(own_col * slab, slab), slab), :]
        lower_ref[:, here] = tile
        gram_in[0] += product(tile, lower, 1, 1)

        @pl.when(q == PIECES - 1)
        def _():
            start_all(gram_copy, row_devices)

        middle = trailing_ref[here, :] - product(prev_full, prev_upper_ref[...], 0, 0)
        trailing_ref[here, :] = middle - product(lower, right_ref[...], 0, 0)
        for copy in piece_copies(q):
            copy.start()

    sent_all(picked_copy, row_devices)
    sent_all(zone_copy, col_devices)
    sent_all(block_copy, row_devices)
    sent_all(trail_copy, row_devices)
    sent_all(trail_out_copy, row_devices)

    @pl.loop(0, PIECES)
    def _(q):
        @pl.loop(0, col_devices)
        def _(source):
            @pl.when((source <= own_col) & (own_col < col_devices - 1))
            def _():
                tall_copy(q, source, 0, own_col + 1).wait_send()

            @pl.when((source >= own_col) & (own_col > 0))
            def _():
                tall_copy(q, source, 1, own_col - 1).wait_send()

    land_all(gram_copy, row_devices)
    total = gram_in[0]
    for d in range(1, row_devices):
        total = total + gram_in[d]
    gram_ref[...] = total / (rows_here * row_devices)
    last = pltpu.make_async_copy(gram_ref, gram_hbm, out_sem.at[2])
    last.start()
    sent_all(gram_copy, row_devices)

    @pl.loop(0, PIECES)
    def _(q):
        for copy in piece_copies(q):
            copy.wait()

    u_copy.wait()
    right_copy.wait()
    last.wait()


def place_kernel(*refs):
    sources, places, sem = refs[:5], refs[5:10], refs[10]
    copies = []
    for source, place in zip(sources, places):
        height = source.shape[0]
        parts = 4 if height >= 1024 else 1
        for part in range(parts):
            rows = pl.ds(part * (height // parts), height // parts)
            copies.append(
                pltpu.make_async_copy(source.at[rows, :], place.at[rows, :], sem.at[len(copies)])
            )
    for copy in copies:
        copy.start()
    for copy in copies:
        copy.wait()


def body(row_devices, col_devices, panel_t, trailing, prev_lower_t, prev_upper, leaf, merge):
    slab, rows_here = panel_t.shape
    order = merge.shape[1]
    trail_cols = trailing.shape[1]
    share = order // row_devices
    span = rows_here // PIECES
    real = jnp.float32
    square = pltpu.VMEM((order, order), real)
    anywhere = pl.BlockSpec(memory_space=pl.ANY)
    dma = pltpu.SemaphoreType.DMA
    shapes = [
        jax.ShapeDtypeStruct((slab, rows_here), real),
        jax.ShapeDtypeStruct((order, order), real),
        jax.ShapeDtypeStruct((order, trail_cols), real),
        jax.ShapeDtypeStruct((rows_here, trail_cols), real),
        jax.ShapeDtypeStruct((slab, order), real),
    ]
    results = pl.pallas_call(
        functools.partial(step_kernel, row_devices, col_devices),
        out_shape=shapes,
        in_specs=[anywhere] * 6,
        out_specs=[anywhere] * 5,
        scratch_shapes=[
            pltpu.VMEM((rows_here, trail_cols), real),
            pltpu.VMEM((order, trail_cols), real),
            pltpu.VMEM((1, order), jnp.int32),
            pltpu.VMEM(merge.shape, jnp.int32),
            pltpu.VMEM((slab, rows_here), real),
            square,
            pltpu.VMEM((order, trail_cols), real),
            pltpu.VMEM((slab, order), real),
            pltpu.VMEM((PIECES, col_devices, 2 * slab, span), real),
            pltpu.VMEM((order, 128), real),
            pltpu.VMEM((row_devices, share, 128), real),
            pltpu.VMEM((row_devices, col_devices, share, 128), real),
            pltpu.VMEM((order, trail_cols), real),
            pltpu.VMEM((row_devices, share, trail_cols), real),
            pltpu.VMEM((row_devices, share, trail_cols), real),
            square,
            square,
            square,
            square,
            pltpu.VMEM((order, span), real),
            pltpu.VMEM((row_devices, slab, order), real),
            dma((2, col_devices, PIECES)),
            dma((col_devices, PIECES)),
            dma((5, row_devices)),
            dma((5, row_devices)),
            dma((col_devices,)),
            dma((col_devices,)),
            dma((2, PIECES)),
            dma((4,)),
            dma((2, PIECES)),
            dma((3,)),
        ],
        compiler_params=pltpu.CompilerParams(
            collective_id=0, has_side_effects=True, vmem_limit_bytes=56 * 1024 * 1024
        ),
        name="panel_step",
    )(panel_t, trailing, prev_lower_t, prev_upper, leaf, merge)
    return pl.pallas_call(
        place_kernel,
        out_shape=shapes,
        in_specs=[anywhere] * 5,
        out_specs=[anywhere] * 5,
        scratch_shapes=[dma((8,))],
        compiler_params=pltpu.CompilerParams(vmem_limit_bytes=56 * 1024 * 1024),
        name="place_outputs",
    )(*results)


def solution(mesh):
    return jax.shard_map(
        functools.partial(body, mesh.shape["rows"], mesh.shape["cols"]),
        mesh=mesh,
        in_specs=(
            P("cols", "rows"),
            P("rows", "cols"),
            P("cols", "rows"),
            P(None, "cols"),
            P("rows", None),
            P(),
        ),
        out_specs=(P("cols", "rows"), P(), P(None, "cols"), P("rows", "cols"), P("cols", None)),
        check_vma=False,
    )
```

```python
import functools
import jax
import jax.numpy as jnp
from jax import lax
from jax.experimental import pallas as pl
from jax.experimental.pallas import tpu as pltpu
from jax.sharding import PartitionSpec as P

MESH = pl.DeviceIdType.MESH
PIECES = 8
HALF = PIECES // 2

BLOCK = 32


def pieces(value):
    first = value.astype(jnp.bfloat16)
    rest = value - first.astype(jnp.float32)
    second = rest.astype(jnp.bfloat16)
    third = (rest - second.astype(jnp.float32)).astype(jnp.bfloat16)
    return first, second, third


def thin_product(left_t, right):
    l0, l1, l2 = pieces(left_t)
    r0, r1, r2 = pieces(right)
    left_stack = jnp.concatenate([l0, l0, l1, l1, l0, l2], 0)
    right_stack = jnp.concatenate([r0, r1, r0, r1, r2, r0], 0)
    return lax.dot_general(
        left_stack, right_stack, (((0,), (0,)), ((), ())), preferred_element_type=jnp.float32
    )


def eliminate(tiles):
    sub = lax.broadcasted_iota(jnp.int32, (8, 128), 0)
    groups = BLOCK // 8
    for k in range(BLOCK - 1):
        home, s = k // 8, k % 8
        for chain in tiles:
            row = [jnp.broadcast_to(t[s : s + 1, :], (8, 128)) for t in chain[home]]
            inverse = 1.0 / row[0]
            for g in range(home, groups):
                if g == home and s == 7:
                    continue
                scaled = chain[g][0] * inverse
                if g == home:
                    scaled = jnp.where(sub > s, scaled, 0.0)
                factor = jnp.broadcast_to(scaled[:, k : k + 1], (8, 128))
                chain[g] = [t - factor * r for t, r in zip(chain[g], row)]
    return tiles


def lu_stage(stage, order, w, x, u_ref, linv_ref, uinvt_ref):
    groups = BLOCK // 8
    start = pl.multiple_of(stage * BLOCK, BLOCK)
    rows = pl.ds(start, BLOCK)
    back = lax.rem(order - start, order)
    spare = order // 128
    lane = lax.broadcasted_iota(jnp.int32, (BLOCK, order), 1)
    sub = lax.broadcasted_iota(jnp.int32, (BLOCK, order), 0)
    eye8 = lax.broadcasted_iota(jnp.int32, (8, 128), 1) - lax.broadcasted_iota(
        jnp.int32, (8, 128), 0
    )
    chains = []
    for ref in (w, x):
        turned = pltpu.roll(ref[rows, :], back, 1)
        chain = []
        for g in range(groups):
            part = [turned[8 * g : 8 * g + 8, 128 * t : 128 * t + 128] for t in range(spare)]
            part.append(jnp.where(eye8 == 8 * g, 1.0, 0.0))
            chain.append(part)
        chains.append(chain)
    chains = eliminate(chains)
    full, joined, diagonal = [], [], []
    for chain in chains:
        main = jnp.concatenate(
            [jnp.concatenate([chain[g][t] for g in range(groups)], 0) for t in range(spare)], 1
        )
        extra = jnp.concatenate([chain[g][spare] for g in range(groups)], 0)
        extra = jnp.concatenate([extra] + [jnp.zeros((BLOCK, 128), jnp.float32)] * (spare - 1), 1)
        pivot = jnp.sum(jnp.where(lane == sub, main, 0.0), 1, keepdims=True)
        mixed = jnp.where(lane < BLOCK, extra, main)
        full.append(pltpu.roll(main, start, 1))
        joined.append(pltpu.roll(mixed, start, 1))
        diagonal.append(pivot)
    u_ref[rows, :] = jnp.where(lane >= sub + start, full[0], 0.0)
    reached = lane < start + BLOCK
    inverse_w = 1.0 / diagonal[0]
    inverse_x = 1.0 / diagonal[1]
    linv_ref[rows, :] = jnp.where(reached, joined[0], 0.0)
    uinvt_ref[rows, :] = jnp.where(reached, joined[1] * inverse_x, 0.0)
    lower = jnp.where(reached, 0.0, full[1] * inverse_x)
    upper = jnp.where(reached, 0.0, full[0] * inverse_w)
    cols = lax.broadcasted_iota(jnp.int32, (order, order), 1)
    inside = (cols >= start) & (cols < start + BLOCK)
    w[...] = jnp.where(inside, 0.0, w[...]) - thin_product(lower, joined[0])
    x[...] = jnp.where(inside, 0.0, x[...]) - thin_product(upper, joined[1])


def halves(value):
    first = value.astype(jnp.bfloat16)
    return first, (value - first.astype(jnp.float32)).astype(jnp.bfloat16)


def product(left, right, left_dim=1, right_dim=0):
    dims = (((left_dim,), (right_dim,)), ((), ()))
    a0, a1 = halves(left)
    b0, b1 = halves(right)
    dot = functools.partial(
        lax.dot_general, dimension_numbers=dims, preferred_element_type=jnp.float32
    )
    return dot(a0, b0) + (dot(a0, b1) + dot(a1, b0))


def trace_rows(merge_ref, leaf_ref, row_devices, own_row):
    width = merge_ref.shape[1]
    lane = lax.broadcasted_iota(jnp.int32, (width, width), 1)
    slot = lax.broadcasted_iota(jnp.int32, (width, 1), 0)
    group = jnp.zeros((width, 1), jnp.int32)

    def look_up(table):
        found = jnp.where(lane == slot, table.astype(jnp.float32), 0.0)
        return jnp.sum(found, 1, keepdims=True).astype(jnp.int32)

    for section in reversed(range(row_devices.bit_length() - 1)):
        offset = row_devices - (row_devices >> section)
        table = jnp.broadcast_to(merge_ref[offset : offset + 1, :], (width, width))
        for g in range(1, row_devices >> (section + 1)):
            line = merge_ref[offset + g : offset + g + 1, :]
            table = jnp.where(group == g, line, table)
        position = look_up(table)
        right_side = (position >= width).astype(jnp.int32)
        group = 2 * group + right_side
        slot = position - width * right_side
    local = look_up(jnp.broadcast_to(leaf_ref[...], (width, width)))
    return jnp.where(group == own_row, local, -1)


def step_kernel(
    row_devices,
    col_devices,
    panel_hbm,
    trailing_hbm,
    prev_hbm,
    prev_upper_hbm,
    leaf_hbm,
    merge_hbm,
    lower_hbm,
    u_hbm,
    right_hbm,
    updated_hbm,
    gram_hbm,
    trailing_ref,
    prev_upper_ref,
    leaf_ref,
    merge_ref,
    lower_ref,
    u_ref,
    right_ref,
    gram_ref,
    tall,
    picked,
    picked_in,
    block,
    trail,
    trail_in,
    trail_all,
    w,
    x,
    linv,
    uinvt,
    lower_full,
    gram_in,
    tall_send,
    tall_recv,
    row_send,
    row_recv,
    zone_send,
    zone_recv,
    own_sem,
    in_sem,
    piece_sem,
    out_sem,
):
    slab, rows_here = panel_hbm.shape
    order = merge_ref.shape[1]
    trail_cols = trailing_ref.shape[1]
    share = order // row_devices
    span = rows_here // HALF
    own_row = lax.axis_index("rows")
    own_col = lax.axis_index("cols")

    barrier = pltpu.get_barrier_semaphore()

    @pl.loop(1, row_devices)
    def _(d):
        pl.semaphore_signal(
            barrier,
            inc=1,
            device_id={"rows": lax.rem(own_row + d, row_devices)},
            device_id_type=MESH,
        )

    @pl.loop(1, col_devices)
    def _(d):
        pl.semaphore_signal(
            barrier,
            inc=1,
            device_id={"cols": lax.rem(own_col + d, col_devices)},
            device_id_type=MESH,
        )

    own_copies = []
    for q in range(PIECES):
        source = panel_hbm if q < HALF else prev_hbm
        part = pl.ds(q % HALF * span, span)
        own_copies.append(
            pltpu.make_async_copy(source.at[:, part], tall.at[q, own_col], own_sem.at[q])
        )
    loads = [
        pltpu.make_async_copy(source, place, in_sem.at[i])
        for i, (source, place) in enumerate(
            (
                (merge_hbm, merge_ref),
                (leaf_hbm, leaf_ref),
                (trailing_hbm, trailing_ref),
                (prev_upper_hbm, prev_upper_ref),
            )
        )
    ]
    for copy in loads[:2] + own_copies + loads[2:]:
        copy.start()
    for copy in own_copies:
        copy.wait()
    pl.semaphore_wait(barrier, row_devices + col_devices - 2)

    def tall_copy(q, source, way, to):
        place = tall.at[q, source]
        return pltpu.make_async_remote_copy(
            src_ref=place,
            dst_ref=place,
            send_sem=tall_send.at[way, source, q],
            recv_sem=tall_recv.at[source, q],
            device_id={"cols": to},
            device_id_type=MESH,
        )

    def step(hop, q):
        up = own_col - hop
        down = own_col + hop
        if hop > 0:

            @pl.when(up >= 0)
            def _():
                tall_copy(q, up, 0, own_col - 1).wait_recv()

        @pl.when((up >= 0) & (own_col < col_devices - 1))
        def _():
            tall_copy(q, up, 0, own_col + 1).start()

        if hop > 0:

            @pl.when(down < col_devices)
            def _():
                tall_copy(q, down, 1, own_col + 1).wait_recv()

        @pl.when((down < col_devices) & (own_col > 0))
        def _():
            tall_copy(q, down, 1, own_col - 1).start()

    def share_of(d):
        return pl.ds(pl.multiple_of(lax.rem(own_row + d, row_devices) * share, share), share)

    def row_copy(kind, d, src, dst):
        return pltpu.make_async_remote_copy(
            src_ref=src,
            dst_ref=dst,
            send_sem=row_send.at[kind, d],
            recv_sem=row_recv.at[kind, d],
            device_id={"rows": lax.rem(own_row + d, row_devices)},
            device_id_type=MESH,
        )

    def picked_copy(d):
        return row_copy(0, d, picked.at[share_of(d), :], picked_in.at[d])

    def block_copy(d):
        return row_copy(1, d, block.at[own_row], block.at[own_row])

    def trail_copy(d):
        return row_copy(2, d, trail.at[share_of(d), :], trail_in.at[d])

    def trail_out_copy(d):
        return row_copy(3, d, trail_all.at[own_row], trail_all.at[own_row])

    def gram_copy(d):
        return row_copy(4, d, gram_in.at[0], gram_in.at[d])

    def zone_copy(d):
        return pltpu.make_async_remote_copy(
            src_ref=block.at[own_row, own_col],
            dst_ref=block.at[own_row, own_col],
            send_sem=zone_send.at[d],
            recv_sem=zone_recv.at[d],
            device_id={"cols": lax.rem(own_col + d, col_devices)},
            device_id_type=MESH,
        )

    def start_all(copy, count):
        @pl.loop(1, count)
        def _(d):
            copy(d).start()

    def land_all(copy, count):
        @pl.loop(1, count)
        def _(d):
            copy(d).wait_recv()

    def sent_all(copy, count):
        @pl.loop(1, count)
        def _(d):
            copy(d).wait_send()

    for q in range(HALF):
        step(0, q)
    loads[0].wait()
    loads[1].wait()
    target = trace_rows(merge_ref, leaf_ref, row_devices, own_row)
    lane = lax.broadcasted_iota(jnp.int32, (order, span), 1)

    def one_hot(q):
        return jnp.where(lane + q * span == target, 1.0, 0.0).astype(jnp.bfloat16)

    total = jnp.zeros((order, 128), jnp.float32)
    for q in range(HALF):
        stack = jnp.concatenate([tall[q, own_col], tall[q + HALF, own_col]], 0)
        if 2 * slab < 128:
            stack = jnp.concatenate([stack, jnp.zeros((128 - 2 * slab, span), jnp.float32)], 0)
        found = lax.dot_general(
            one_hot(q),
            jnp.concatenate(pieces(stack), 0),
            (((1,), (1,)), ((), ())),
            preferred_element_type=jnp.float32,
        )
        total = total + (found[:, :128] + found[:, 128:256] + found[:, 256:])
    picked[...] = total
    start_all(picked_copy, row_devices)
    loads[2].wait()
    loads[3].wait()

    total = jnp.zeros((order, trail_cols), jnp.float32)
    for q in range(HALF):
        chosen = one_hot(q)
        for part in pieces(trailing_ref[q * span : (q + 1) * span, :]):
            total = total + jnp.dot(chosen, part, preferred_element_type=jnp.float32)
    trail[...] = total

    land_all(picked_copy, row_devices)
    total = picked[share_of(0), :]
    for d in range(1, row_devices):
        total = total + picked_in[d]
    block[own_row, own_col] = total
    start_all(zone_copy, col_devices)
    land_all(zone_copy, col_devices)
    start_all(block_copy, row_devices)
    start_all(trail_copy, row_devices)
    for q in range(HALF, PIECES):
        step(0, q)
    land_all(block_copy, row_devices)

    def gathered(first):
        parts = []
        for z in range(col_devices):
            parts.append(block[:, z].reshape(order, 128)[:, first : first + slab])
        return jnp.concatenate(parts, 1)

    matrix = gathered(0)
    w[...] = matrix
    x[...] = matrix.T

    count = order // BLOCK

    @pl.loop(0, count)
    def _(stage):
        lu_stage(stage, order, w, x, u_ref, linv, uinvt)
        for part in range(PIECES // count):
            step(1, stage * (PIECES // count) + part)

        @pl.when(stage == 2)
        def _():
            land_all(trail_copy, row_devices)
            total = trail[share_of(0), :]
            for d in range(1, row_devices):
                total = total + trail_in[d]
            trail_all[own_row] = total
            start_all(trail_out_copy, row_devices)

    land_all(trail_out_copy, row_devices)
    chosen = trail_all[...].reshape(order, trail_cols)
    chosen = chosen - product(gathered(slab), prev_upper_ref[...])
    right_ref[...] = product(linv[...], chosen)
    gram_in[0] = jnp.zeros((slab, order), jnp.float32)
    u_copy = pltpu.make_async_copy(u_ref, u_hbm, out_sem.at[0])
    right_copy = pltpu.make_async_copy(right_ref, right_hbm, out_sem.at[1])
    u_copy.start()
    right_copy.start()
    for hop in range(2, col_devices - 1):

        @pl.loop(0, PIECES)
        def _(q):
            step(hop, q)

    def piece_copies(q):
        here = pl.ds(pl.multiple_of(q * span, span), span)
        return (
            pltpu.make_async_copy(lower_ref.at[:, here], lower_hbm.at[:, here], piece_sem.at[0, q]),
            pltpu.make_async_copy(
                trailing_ref.at[here, :], updated_hbm.at[here, :], piece_sem.at[1, q]
            ),
        )

    @pl.loop(0, HALF)
    def _(q):
        step(col_devices - 1, q)
        here = pl.ds(pl.multiple_of(q * span, span), span)
        lower = product(uinvt[...], tall[q].reshape(order, span))
        lower_full[q] = lower
        tile = lower_full[q, pl.ds(pl.multiple_of(own_col * slab, slab), slab), :]
        lower_ref[:, here] = tile
        piece_copies(q)[0].start()
        gram_in[0] += product(tile, lower, 1, 1)

        @pl.when(q == HALF - 1)
        def _():
            start_all(gram_copy, row_devices)

        trailing_ref[here, :] = trailing_ref[here, :] - product(lower, right_ref[...], 0, 0)

    last = pltpu.make_async_copy(gram_ref, gram_hbm, out_sem.at[2])

    @pl.loop(0, HALF)
    def _(q):
        @pl.when(q == HALF - 1)
        def _():
            land_all(gram_copy, row_devices)
            total = gram_in[0]
            for d in range(1, row_devices):
                total = total + gram_in[d]
            gram_ref[...] = total / (rows_here * row_devices)
            last.start()

        step(col_devices - 1, q + HALF)
        here = pl.ds(pl.multiple_of(q * span, span), span)
        prev_full = tall[q + HALF].reshape(order, span)
        trailing_ref[here, :] = trailing_ref[here, :] - product(
            prev_full, prev_upper_ref[...], 0, 0
        )
        piece_copies(q)[1].start()

    sent_all(picked_copy, row_devices)
    sent_all(zone_copy, col_devices)
    sent_all(block_copy, row_devices)
    sent_all(trail_copy, row_devices)
    sent_all(trail_out_copy, row_devices)

    @pl.loop(0, PIECES)
    def _(q):
        @pl.loop(0, col_devices)
        def _(source):
            @pl.when((source <= own_col) & (own_col < col_devices - 1))
            def _():
                tall_copy(q, source, 0, own_col + 1).wait_send()

            @pl.when((source >= own_col) & (own_col > 0))
            def _():
                tall_copy(q, source, 1, own_col - 1).wait_send()

    sent_all(gram_copy, row_devices)

    @pl.loop(0, HALF)
    def _(q):
        for copy in piece_copies(q):
            copy.wait()

    u_copy.wait()
    right_copy.wait()
    last.wait()


def place_kernel(*refs):
    sources, places, held, in_sem, out_sem = refs[:5], refs[5:10], refs[10:15], refs[15], refs[16]
    arrivals, departures = [], []
    for source, place, middle in zip(sources, places, held):
        height = source.shape[0]
        parts = 4 if height >= 1024 else 1
        for part in range(parts):
            rows = pl.ds(part * (height // parts), height // parts)
            here = middle.at[rows, :]
            index = len(arrivals)
            arrivals.append(pltpu.make_async_copy(source.at[rows, :], here, in_sem.at[index]))
            departures.append(pltpu.make_async_copy(here, place.at[rows, :], out_sem.at[index]))
    for copy in arrivals:
        copy.start()
    for arrival, departure in zip(arrivals, departures):
        arrival.wait()
        departure.start()
    for copy in departures:
        copy.wait()


def body(row_devices, col_devices, panel_t, trailing, prev_lower_t, prev_upper, leaf, merge):
    slab, rows_here = panel_t.shape
    order = merge.shape[1]
    trail_cols = trailing.shape[1]
    share = order // row_devices
    span = rows_here // HALF
    real = jnp.float32
    square = pltpu.VMEM((order, order), real)
    anywhere = pl.BlockSpec(memory_space=pl.ANY)
    dma = pltpu.SemaphoreType.DMA
    shapes = [
        jax.ShapeDtypeStruct((slab, rows_here), real),
        jax.ShapeDtypeStruct((order, order), real),
        jax.ShapeDtypeStruct((order, trail_cols), real),
        jax.ShapeDtypeStruct((rows_here, trail_cols), real),
        jax.ShapeDtypeStruct((slab, order), real),
    ]
    results = pl.pallas_call(
        functools.partial(step_kernel, row_devices, col_devices),
        out_shape=shapes,
        in_specs=[anywhere] * 6,
        out_specs=[anywhere] * 5,
        scratch_shapes=[
            pltpu.VMEM((rows_here, trail_cols), real),
            pltpu.VMEM((order, trail_cols), real),
            pltpu.VMEM((1, order), jnp.int32),
            pltpu.VMEM(merge.shape, jnp.int32),
            pltpu.VMEM((slab, rows_here), real),
            square,
            pltpu.VMEM((order, trail_cols), real),
            pltpu.VMEM((slab, order), real),
            pltpu.VMEM((PIECES, col_devices, slab, span), real),
            pltpu.VMEM((order, 128), real),
            pltpu.VMEM((row_devices, share, 128), real),
            pltpu.VMEM((row_devices, col_devices, share, 128), real),
            pltpu.VMEM((order, trail_cols), real),
            pltpu.VMEM((row_devices, share, trail_cols), real),
            pltpu.VMEM((row_devices, share, trail_cols), real),
            square,
            square,
            square,
            square,
            pltpu.VMEM((HALF, order, span), real),
            pltpu.VMEM((row_devices, slab, order), real),
            dma((2, col_devices, PIECES)),
            dma((col_devices, PIECES)),
            dma((5, row_devices)),
            dma((5, row_devices)),
            dma((col_devices,)),
            dma((col_devices,)),
            dma((PIECES,)),
            dma((4,)),
            dma((2, HALF)),
            dma((3,)),
        ],
        compiler_params=pltpu.CompilerParams(
            collective_id=0, has_side_effects=True, vmem_limit_bytes=56 * 1024 * 1024
        ),
        name="panel_step",
    )(panel_t, trailing, prev_lower_t, prev_upper, leaf, merge)
    return pl.pallas_call(
        place_kernel,
        out_shape=shapes,
        in_specs=[anywhere] * 5,
        out_specs=[anywhere] * 5,
        scratch_shapes=[pltpu.VMEM(shape.shape, real) for shape in shapes] + [dma((8,))] * 2,
        compiler_params=pltpu.CompilerParams(vmem_limit_bytes=56 * 1024 * 1024),
        name="place_outputs",
    )(*results)


def solution(mesh):
    return jax.shard_map(
        functools.partial(body, mesh.shape["rows"], mesh.shape["cols"]),
        mesh=mesh,
        in_specs=(
            P("cols", "rows"),
            P("rows", "cols"),
            P("cols", "rows"),
            P(None, "cols"),
            P("rows", None),
            P(),
        ),
        out_specs=(P("cols", "rows"), P(), P(None, "cols"), P("rows", "cols"), P("cols", None)),
        check_vma=False,
    )
```

```python
import functools
import jax
import jax.numpy as jnp
from jax import lax
from jax.experimental import pallas as pl
from jax.experimental.pallas import tpu as pltpu
from jax.sharding import PartitionSpec as P

MESH = pl.DeviceIdType.MESH
PIECES = 8
HALF = PIECES // 2

BLOCK = 32


def pieces(value):
    first = value.astype(jnp.bfloat16)
    rest = value - first.astype(jnp.float32)
    second = rest.astype(jnp.bfloat16)
    third = (rest - second.astype(jnp.float32)).astype(jnp.bfloat16)
    return first, second, third


def thin_product(left_t, right):
    l0, l1, l2 = pieces(left_t)
    r0, r1, r2 = pieces(right)
    left_stack = jnp.concatenate([l0, l0, l1, l1, l0, l2], 0)
    right_stack = jnp.concatenate([r0, r1, r0, r1, r2, r0], 0)
    return lax.dot_general(
        left_stack, right_stack, (((0,), (0,)), ((), ())), preferred_element_type=jnp.float32
    )


def eliminate(tiles):
    sub = lax.broadcasted_iota(jnp.int32, (8, 128), 0)
    groups = BLOCK // 8
    for k in range(BLOCK - 1):
        home, s = k // 8, k % 8
        for chain in tiles:
            row = [jnp.broadcast_to(t[s : s + 1, :], (8, 128)) for t in chain[home]]
            inverse = 1.0 / row[0]
            for g in range(home, groups):
                if g == home and s == 7:
                    continue
                scaled = chain[g][0] * inverse
                if g == home:
                    scaled = jnp.where(sub > s, scaled, 0.0)
                factor = jnp.broadcast_to(scaled[:, k : k + 1], (8, 128))
                chain[g] = [t - factor * r for t, r in zip(chain[g], row)]
    return tiles


def lu_stage(stage, order, w, x, u_ref, linv_ref, uinvt_ref):
    groups = BLOCK // 8
    start = pl.multiple_of(stage * BLOCK, BLOCK)
    rows = pl.ds(start, BLOCK)
    back = lax.rem(order - start, order)
    spare = order // 128
    lane = lax.broadcasted_iota(jnp.int32, (BLOCK, order), 1)
    sub = lax.broadcasted_iota(jnp.int32, (BLOCK, order), 0)
    eye8 = lax.broadcasted_iota(jnp.int32, (8, 128), 1) - lax.broadcasted_iota(
        jnp.int32, (8, 128), 0
    )
    chains = []
    for ref in (w, x):
        turned = pltpu.roll(ref[rows, :], back, 1)
        chain = []
        for g in range(groups):
            part = [turned[8 * g : 8 * g + 8, 128 * t : 128 * t + 128] for t in range(spare)]
            part.append(jnp.where(eye8 == 8 * g, 1.0, 0.0))
            chain.append(part)
        chains.append(chain)
    chains = eliminate(chains)
    full, joined, diagonal = [], [], []
    for chain in chains:
        main = jnp.concatenate(
            [jnp.concatenate([chain[g][t] for g in range(groups)], 0) for t in range(spare)], 1
        )
        extra = jnp.concatenate([chain[g][spare] for g in range(groups)], 0)
        extra = jnp.concatenate([extra] + [jnp.zeros((BLOCK, 128), jnp.float32)] * (spare - 1), 1)
        pivot = jnp.sum(jnp.where(lane == sub, main, 0.0), 1, keepdims=True)
        mixed = jnp.where(lane < BLOCK, extra, main)
        full.append(pltpu.roll(main, start, 1))
        joined.append(pltpu.roll(mixed, start, 1))
        diagonal.append(pivot)
    u_ref[rows, :] = jnp.where(lane >= sub + start, full[0], 0.0)
    reached = lane < start + BLOCK
    inverse_w = 1.0 / diagonal[0]
    inverse_x = 1.0 / diagonal[1]
    linv_ref[rows, :] = jnp.where(reached, joined[0], 0.0)
    uinvt_ref[rows, :] = jnp.where(reached, joined[1] * inverse_x, 0.0)
    lower = jnp.where(reached, 0.0, full[1] * inverse_x)
    upper = jnp.where(reached, 0.0, full[0] * inverse_w)
    cols = lax.broadcasted_iota(jnp.int32, (order, order), 1)
    inside = (cols >= start) & (cols < start + BLOCK)
    w[...] = jnp.where(inside, 0.0, w[...]) - thin_product(lower, joined[0])
    x[...] = jnp.where(inside, 0.0, x[...]) - thin_product(upper, joined[1])


def halves(value):
    first = value.astype(jnp.bfloat16)
    return first, (value - first.astype(jnp.float32)).astype(jnp.bfloat16)


def product(left, right, left_dim=1, right_dim=0):
    dims = (((left_dim,), (right_dim,)), ((), ()))
    a0, a1 = halves(left)
    b0, b1 = halves(right)
    dot = functools.partial(
        lax.dot_general, dimension_numbers=dims, preferred_element_type=jnp.float32
    )
    return dot(a0, b0) + (dot(a0, b1) + dot(a1, b0))


def trace_rows(merge_ref, leaf_ref, row_devices, own_row):
    width = merge_ref.shape[1]
    lane = lax.broadcasted_iota(jnp.int32, (width, width), 1)
    slot = lax.broadcasted_iota(jnp.int32, (width, 1), 0)
    group = jnp.zeros((width, 1), jnp.int32)

    def look_up(table):
        found = jnp.where(lane == slot, table.astype(jnp.float32), 0.0)
        return jnp.sum(found, 1, keepdims=True).astype(jnp.int32)

    for section in reversed(range(row_devices.bit_length() - 1)):
        offset = row_devices - (row_devices >> section)
        table = jnp.broadcast_to(merge_ref[offset : offset + 1, :], (width, width))
        for g in range(1, row_devices >> (section + 1)):
            line = merge_ref[offset + g : offset + g + 1, :]
            table = jnp.where(group == g, line, table)
        position = look_up(table)
        right_side = (position >= width).astype(jnp.int32)
        group = 2 * group + right_side
        slot = position - width * right_side
    local = look_up(jnp.broadcast_to(leaf_ref[...], (width, width)))
    return jnp.where(group == own_row, local, -1)


def step_kernel(
    row_devices,
    col_devices,
    panel_hbm,
    trailing_hbm,
    prev_hbm,
    prev_upper_hbm,
    leaf_hbm,
    merge_hbm,
    lower_hbm,
    u_hbm,
    right_hbm,
    updated_hbm,
    gram_hbm,
    trailing_ref,
    prev_upper_ref,
    leaf_ref,
    merge_ref,
    lower_ref,
    u_ref,
    right_ref,
    gram_ref,
    tall,
    picked,
    picked_in,
    block,
    trail,
    trail_in,
    trail_all,
    w,
    x,
    linv,
    uinvt,
    lower_full,
    gram_in,
    tall_send,
    tall_recv,
    row_send,
    row_recv,
    zone_send,
    zone_recv,
    own_sem,
    in_sem,
    piece_sem,
    out_sem,
):
    slab, rows_here = panel_hbm.shape
    order = merge_ref.shape[1]
    trail_cols = trailing_ref.shape[1]
    share = order // row_devices
    span = rows_here // HALF
    own_row = lax.axis_index("rows")
    own_col = lax.axis_index("cols")

    barrier = pltpu.get_barrier_semaphore()

    @pl.loop(1, row_devices)
    def _(d):
        pl.semaphore_signal(
            barrier,
            inc=1,
            device_id={"rows": lax.rem(own_row + d, row_devices)},
            device_id_type=MESH,
        )

    @pl.loop(1, col_devices)
    def _(d):
        pl.semaphore_signal(
            barrier,
            inc=1,
            device_id={"cols": lax.rem(own_col + d, col_devices)},
            device_id_type=MESH,
        )

    own_copies = []
    for q in range(PIECES):
        source = panel_hbm if q < HALF else prev_hbm
        part = pl.ds(q % HALF * span, span)
        own_copies.append(
            pltpu.make_async_copy(source.at[:, part], tall.at[q, own_col], own_sem.at[q])
        )
    loads = [
        pltpu.make_async_copy(source, place, in_sem.at[i])
        for i, (source, place) in enumerate(
            (
                (merge_hbm, merge_ref),
                (leaf_hbm, leaf_ref),
                (trailing_hbm, trailing_ref),
                (prev_upper_hbm, prev_upper_ref),
            )
        )
    ]
    for copy in loads[:2] + own_copies + loads[2:]:
        copy.start()
    for copy in own_copies:
        copy.wait()
    pl.semaphore_wait(barrier, row_devices + col_devices - 2)

    def tall_copy(q, source, way, to):
        place = tall.at[q, source]
        return pltpu.make_async_remote_copy(
            src_ref=place,
            dst_ref=place,
            send_sem=tall_send.at[way, source, q],
            recv_sem=tall_recv.at[source, q],
            device_id={"cols": to},
            device_id_type=MESH,
        )

    def step(hop, q):
        up = own_col - hop
        down = own_col + hop
        if hop > 0:

            @pl.when(up >= 0)
            def _():
                tall_copy(q, up, 0, own_col - 1).wait_recv()

        @pl.when((up >= 0) & (own_col < col_devices - 1))
        def _():
            tall_copy(q, up, 0, own_col + 1).start()

        if hop > 0:

            @pl.when(down < col_devices)
            def _():
                tall_copy(q, down, 1, own_col + 1).wait_recv()

        @pl.when((down < col_devices) & (own_col > 0))
        def _():
            tall_copy(q, down, 1, own_col - 1).start()

    def share_of(d):
        return pl.ds(pl.multiple_of(lax.rem(own_row + d, row_devices) * share, share), share)

    def row_copy(kind, d, src, dst):
        return pltpu.make_async_remote_copy(
            src_ref=src,
            dst_ref=dst,
            send_sem=row_send.at[kind, d],
            recv_sem=row_recv.at[kind, d],
            device_id={"rows": lax.rem(own_row + d, row_devices)},
            device_id_type=MESH,
        )

    def picked_copy(d):
        return row_copy(0, d, picked.at[share_of(d), :], picked_in.at[d])

    def block_copy(d):
        return row_copy(1, d, block.at[own_row], block.at[own_row])

    def trail_copy(d):
        return row_copy(2, d, trail.at[share_of(d), :], trail_in.at[d])

    def trail_out_copy(d):
        return row_copy(3, d, trail_all.at[own_row], trail_all.at[own_row])

    def gram_copy(d):
        return row_copy(4, d, gram_in.at[0], gram_in.at[d])

    def zone_copy(d):
        return pltpu.make_async_remote_copy(
            src_ref=block.at[own_row, own_col],
            dst_ref=block.at[own_row, own_col],
            send_sem=zone_send.at[d],
            recv_sem=zone_recv.at[d],
            device_id={"cols": lax.rem(own_col + d, col_devices)},
            device_id_type=MESH,
        )

    def start_all(copy, count):
        @pl.loop(1, count)
        def _(d):
            copy(d).start()

    def land_all(copy, count):
        @pl.loop(1, count)
        def _(d):
            copy(d).wait_recv()

    def sent_all(copy, count):
        @pl.loop(1, count)
        def _(d):
            copy(d).wait_send()

    for q in range(HALF):
        step(0, q)
    loads[0].wait()
    loads[1].wait()
    target = trace_rows(merge_ref, leaf_ref, row_devices, own_row)
    lane = lax.broadcasted_iota(jnp.int32, (order, span), 1)

    def one_hot(q):
        return jnp.where(lane + q * span == target, 1.0, 0.0).astype(jnp.bfloat16)

    total = jnp.zeros((order, 128), jnp.float32)
    for q in range(HALF):
        stack = jnp.concatenate([tall[q, own_col], tall[q + HALF, own_col]], 0)
        if 2 * slab < 128:
            stack = jnp.concatenate([stack, jnp.zeros((128 - 2 * slab, span), jnp.float32)], 0)
        found = lax.dot_general(
            one_hot(q),
            jnp.concatenate(pieces(stack), 0),
            (((1,), (1,)), ((), ())),
            preferred_element_type=jnp.float32,
        )
        total = total + (found[:, :128] + found[:, 128:256] + found[:, 256:])
    picked[...] = total
    start_all(picked_copy, row_devices)
    loads[2].wait()
    loads[3].wait()

    total = jnp.zeros((order, trail_cols), jnp.float32)
    for q in range(HALF):
        chosen = one_hot(q)
        for part in pieces(trailing_ref[q * span : (q + 1) * span, :]):
            total = total + jnp.dot(chosen, part, preferred_element_type=jnp.float32)
    trail[...] = total

    land_all(picked_copy, row_devices)
    total = picked[share_of(0), :]
    for d in range(1, row_devices):
        total = total + picked_in[d]
    block[own_row, own_col] = total
    start_all(zone_copy, col_devices)
    for q in range(HALF, HALF + 2):
        step(0, q)
    land_all(zone_copy, col_devices)
    start_all(block_copy, row_devices)
    start_all(trail_copy, row_devices)
    for q in range(HALF + 2, PIECES):
        step(0, q)
    land_all(block_copy, row_devices)

    def gathered(first):
        parts = []
        for z in range(col_devices):
            parts.append(block[:, z].reshape(order, 128)[:, first : first + slab])
        return jnp.concatenate(parts, 1)

    matrix = gathered(0)
    w[...] = matrix
    x[...] = matrix.T

    count = order // BLOCK
    early = PIECES // (count // 2)

    @pl.loop(0, count)
    def _(stage):
        lu_stage(stage, order, w, x, u_ref, linv, uinvt)

        @pl.when(stage < count // 2)
        def _():
            for part in range(early):
                step(1, stage * early + part)

        @pl.when(stage >= count // 2)
        def _():
            step(2, stage - count // 2)

        @pl.when(stage == 2)
        def _():
            land_all(trail_copy, row_devices)
            total = trail[share_of(0), :]
            for d in range(1, row_devices):
                total = total + trail_in[d]
            trail_all[own_row] = total
            start_all(trail_out_copy, row_devices)

    land_all(trail_out_copy, row_devices)
    chosen = trail_all[...].reshape(order, trail_cols)
    chosen = chosen - product(gathered(slab), prev_upper_ref[...])
    right_ref[...] = product(linv[...], chosen)
    gram_in[0] = jnp.zeros((slab, order), jnp.float32)
    u_copy = pltpu.make_async_copy(u_ref, u_hbm, out_sem.at[0])
    right_copy = pltpu.make_async_copy(right_ref, right_hbm, out_sem.at[1])
    u_copy.start()
    right_copy.start()
    for hop in range(2, col_devices - 1):

        @pl.loop(count // 2 if hop == 2 else 0, PIECES)
        def _(q):
            step(hop, q)

    def piece_copies(q):
        here = pl.ds(pl.multiple_of(q * span, span), span)
        return (
            pltpu.make_async_copy(lower_ref.at[:, here], lower_hbm.at[:, here], piece_sem.at[0, q]),
            pltpu.make_async_copy(
                trailing_ref.at[here, :], updated_hbm.at[here, :], piece_sem.at[1, q]
            ),
        )

    @pl.loop(0, HALF)
    def _(q):
        step(col_devices - 1, q)
        here = pl.ds(pl.multiple_of(q * span, span), span)
        lower = product(uinvt[...], tall[q].reshape(order, span))
        lower_full[q] = lower
        tile = lower_full[q, pl.ds(pl.multiple_of(own_col * slab, slab), slab), :]
        lower_ref[:, here] = tile
        piece_copies(q)[0].start()
        gram_in[0] += product(tile, lower, 1, 1)

        @pl.when(q == HALF - 1)
        def _():
            start_all(gram_copy, row_devices)

        trailing_ref[here, :] = trailing_ref[here, :] - product(lower, right_ref[...], 0, 0)

    def last_copy():
        return pltpu.make_async_copy(gram_ref, gram_hbm, out_sem.at[2])

    @pl.loop(0, HALF)
    def _(q):
        @pl.when(q == HALF - 1)
        def _():
            land_all(gram_copy, row_devices)
            total = gram_in[0]
            for d in range(1, row_devices):
                total = total + gram_in[d]
            gram_ref[...] = total / (rows_here * row_devices)
            last_copy().start()

        step(col_devices - 1, q + HALF)
        here = pl.ds(pl.multiple_of(q * span, span), span)
        prev_full = tall[q + HALF].reshape(order, span)
        trailing_ref[here, :] = trailing_ref[here, :] - product(
            prev_full, prev_upper_ref[...], 0, 0
        )
        piece_copies(q)[1].start()

    sent_all(picked_copy, row_devices)
    sent_all(zone_copy, col_devices)
    sent_all(block_copy, row_devices)
    sent_all(trail_copy, row_devices)
    sent_all(trail_out_copy, row_devices)

    @pl.loop(0, PIECES)
    def _(q):
        @pl.loop(0, col_devices)
        def _(source):
            @pl.when((source <= own_col) & (own_col < col_devices - 1))
            def _():
                tall_copy(q, source, 0, own_col + 1).wait_send()

            @pl.when((source >= own_col) & (own_col > 0))
            def _():
                tall_copy(q, source, 1, own_col - 1).wait_send()

    sent_all(gram_copy, row_devices)

    @pl.loop(0, HALF)
    def _(q):
        for copy in piece_copies(q):
            copy.wait()

    u_copy.wait()
    right_copy.wait()
    last_copy().wait()


def place_kernel(*refs):
    sources, places, held, in_sem, out_sem = refs[:5], refs[5:10], refs[10:15], refs[15], refs[16]
    arrivals, departures = [], []
    for source, place, middle in zip(sources, places, held):
        height = source.shape[0]
        parts = 4 if height >= 1024 else 1
        for part in range(parts):
            rows = pl.ds(part * (height // parts), height // parts)
            here = middle.at[rows, :]
            index = len(arrivals)
            arrivals.append(pltpu.make_async_copy(source.at[rows, :], here, in_sem.at[index]))
            departures.append(pltpu.make_async_copy(here, place.at[rows, :], out_sem.at[index]))
    for copy in arrivals:
        copy.start()
    for arrival, departure in zip(arrivals, departures):
        arrival.wait()
        departure.start()
    for copy in departures:
        copy.wait()


def body(row_devices, col_devices, panel_t, trailing, prev_lower_t, prev_upper, leaf, merge):
    slab, rows_here = panel_t.shape
    order = merge.shape[1]
    trail_cols = trailing.shape[1]
    share = order // row_devices
    span = rows_here // HALF
    real = jnp.float32
    square = pltpu.VMEM((order, order), real)
    anywhere = pl.BlockSpec(memory_space=pl.ANY)
    dma = pltpu.SemaphoreType.DMA
    shapes = [
        jax.ShapeDtypeStruct((slab, rows_here), real),
        jax.ShapeDtypeStruct((order, order), real),
        jax.ShapeDtypeStruct((order, trail_cols), real),
        jax.ShapeDtypeStruct((rows_here, trail_cols), real),
        jax.ShapeDtypeStruct((slab, order), real),
    ]
    results = pl.pallas_call(
        functools.partial(step_kernel, row_devices, col_devices),
        out_shape=shapes,
        in_specs=[anywhere] * 6,
        out_specs=[anywhere] * 5,
        scratch_shapes=[
            pltpu.VMEM((rows_here, trail_cols), real),
            pltpu.VMEM((order, trail_cols), real),
            pltpu.VMEM((1, order), jnp.int32),
            pltpu.VMEM(merge.shape, jnp.int32),
            pltpu.VMEM((slab, rows_here), real),
            square,
            pltpu.VMEM((order, trail_cols), real),
            pltpu.VMEM((slab, order), real),
            pltpu.VMEM((PIECES, col_devices, slab, span), real),
            pltpu.VMEM((order, 128), real),
            pltpu.VMEM((row_devices, share, 128), real),
            pltpu.VMEM((row_devices, col_devices, share, 128), real),
            pltpu.VMEM((order, trail_cols), real),
            pltpu.VMEM((row_devices, share, trail_cols), real),
            pltpu.VMEM((row_devices, share, trail_cols), real),
            square,
            square,
            square,
            square,
            pltpu.VMEM((HALF, order, span), real),
            pltpu.VMEM((row_devices, slab, order), real),
            dma((2, col_devices, PIECES)),
            dma((col_devices, PIECES)),
            dma((5, row_devices)),
            dma((5, row_devices)),
            dma((col_devices,)),
            dma((col_devices,)),
            dma((PIECES,)),
            dma((4,)),
            dma((2, HALF)),
            dma((3,)),
        ],
        compiler_params=pltpu.CompilerParams(
            collective_id=0, has_side_effects=True, vmem_limit_bytes=56 * 1024 * 1024
        ),
        name="panel_step",
    )(panel_t, trailing, prev_lower_t, prev_upper, leaf, merge)
    return pl.pallas_call(
        place_kernel,
        out_shape=shapes,
        in_specs=[anywhere] * 5,
        out_specs=[anywhere] * 5,
        scratch_shapes=[pltpu.VMEM(shape.shape, real) for shape in shapes] + [dma((8,))] * 2,
        compiler_params=pltpu.CompilerParams(vmem_limit_bytes=56 * 1024 * 1024),
        name="place_outputs",
    )(*results)


def solution(mesh):
    return jax.shard_map(
        functools.partial(body, mesh.shape["rows"], mesh.shape["cols"]),
        mesh=mesh,
        in_specs=(
            P("cols", "rows"),
            P("rows", "cols"),
            P("cols", "rows"),
            P(None, "cols"),
            P("rows", None),
            P(),
        ),
        out_specs=(P("cols", "rows"), P(), P(None, "cols"), P("rows", "cols"), P("cols", None)),
        check_vma=False,
    )
```

```python
import functools
import jax
import jax.numpy as jnp
from jax import lax
from jax.experimental import pallas as pl
from jax.experimental.pallas import tpu as pltpu
from jax.sharding import PartitionSpec as P

MESH = pl.DeviceIdType.MESH
PIECES = 8
HALF = PIECES // 2

BLOCK = 32


def pieces(value):
    first = value.astype(jnp.bfloat16)
    rest = value - first.astype(jnp.float32)
    second = rest.astype(jnp.bfloat16)
    third = (rest - second.astype(jnp.float32)).astype(jnp.bfloat16)
    return first, second, third


def thin_product(left_t, right):
    l0, l1, l2 = pieces(left_t)
    r0, r1, r2 = pieces(right)
    left_stack = jnp.concatenate([l0, l0, l1, l1, l0, l2], 0)
    right_stack = jnp.concatenate([r0, r1, r0, r1, r2, r0], 0)
    return lax.dot_general(
        left_stack, right_stack, (((0,), (0,)), ((), ())), preferred_element_type=jnp.float32
    )


def eliminate(tiles):
    sub = lax.broadcasted_iota(jnp.int32, (8, 128), 0)
    groups = BLOCK // 8
    for k in range(BLOCK - 1):
        home, s = k // 8, k % 8
        for chain in tiles:
            row = [jnp.broadcast_to(t[s : s + 1, :], (8, 128)) for t in chain[home]]
            inverse = 1.0 / row[0]
            for g in range(home, groups):
                if g == home and s == 7:
                    continue
                scaled = chain[g][0] * inverse
                if g == home:
                    scaled = jnp.where(sub > s, scaled, 0.0)
                factor = jnp.broadcast_to(scaled[:, k : k + 1], (8, 128))
                chain[g] = [t - factor * r for t, r in zip(chain[g], row)]
    return tiles


def lu_stage(stage, order, w, x, u_ref, linv_ref, uinvt_ref):
    groups = BLOCK // 8
    start = pl.multiple_of(stage * BLOCK, BLOCK)
    rows = pl.ds(start, BLOCK)
    back = lax.rem(order - start, order)
    spare = order // 128
    lane = lax.broadcasted_iota(jnp.int32, (BLOCK, order), 1)
    sub = lax.broadcasted_iota(jnp.int32, (BLOCK, order), 0)
    eye8 = lax.broadcasted_iota(jnp.int32, (8, 128), 1) - lax.broadcasted_iota(
        jnp.int32, (8, 128), 0
    )
    chains = []
    for ref in (w, x):
        turned = pltpu.roll(ref[rows, :], back, 1)
        chain = []
        for g in range(groups):
            part = [turned[8 * g : 8 * g + 8, 128 * t : 128 * t + 128] for t in range(spare)]
            part.append(jnp.where(eye8 == 8 * g, 1.0, 0.0))
            chain.append(part)
        chains.append(chain)
    chains = eliminate(chains)
    full, joined, diagonal = [], [], []
    for chain in chains:
        main = jnp.concatenate(
            [jnp.concatenate([chain[g][t] for g in range(groups)], 0) for t in range(spare)], 1
        )
        extra = jnp.concatenate([chain[g][spare] for g in range(groups)], 0)
        extra = jnp.concatenate([extra] + [jnp.zeros((BLOCK, 128), jnp.float32)] * (spare - 1), 1)
        pivot = jnp.sum(jnp.where(lane == sub, main, 0.0), 1, keepdims=True)
        mixed = jnp.where(lane < BLOCK, extra, main)
        full.append(pltpu.roll(main, start, 1))
        joined.append(pltpu.roll(mixed, start, 1))
        diagonal.append(pivot)
    u_ref[rows, :] = jnp.where(lane >= sub + start, full[0], 0.0)
    reached = lane < start + BLOCK
    inverse_w = 1.0 / diagonal[0]
    inverse_x = 1.0 / diagonal[1]
    linv_ref[rows, :] = jnp.where(reached, joined[0], 0.0)
    uinvt_ref[rows, :] = jnp.where(reached, joined[1] * inverse_x, 0.0)
    lower = jnp.where(reached, 0.0, full[1] * inverse_x)
    upper = jnp.where(reached, 0.0, full[0] * inverse_w)
    cols = lax.broadcasted_iota(jnp.int32, (order, order), 1)
    inside = (cols >= start) & (cols < start + BLOCK)
    w[...] = jnp.where(inside, 0.0, w[...]) - thin_product(lower, joined[0])
    x[...] = jnp.where(inside, 0.0, x[...]) - thin_product(upper, joined[1])


def halves(value):
    first = value.astype(jnp.bfloat16)
    return first, (value - first.astype(jnp.float32)).astype(jnp.bfloat16)


def product(left, right, left_dim=1, right_dim=0):
    dims = (((left_dim,), (right_dim,)), ((), ()))
    a0, a1 = halves(left)
    b0, b1 = halves(right)
    dot = functools.partial(
        lax.dot_general, dimension_numbers=dims, preferred_element_type=jnp.float32
    )
    return dot(a0, b0) + (dot(a0, b1) + dot(a1, b0))


def trace_rows(merge_ref, leaf_ref, row_devices, own_row):
    width = merge_ref.shape[1]
    lane = lax.broadcasted_iota(jnp.int32, (width, width), 1)
    slot = lax.broadcasted_iota(jnp.int32, (width, 1), 0)
    group = jnp.zeros((width, 1), jnp.int32)

    def look_up(table):
        found = jnp.where(lane == slot, table.astype(jnp.float32), 0.0)
        return jnp.sum(found, 1, keepdims=True).astype(jnp.int32)

    for section in reversed(range(row_devices.bit_length() - 1)):
        offset = row_devices - (row_devices >> section)
        table = jnp.broadcast_to(merge_ref[offset : offset + 1, :], (width, width))
        for g in range(1, row_devices >> (section + 1)):
            line = merge_ref[offset + g : offset + g + 1, :]
            table = jnp.where(group == g, line, table)
        position = look_up(table)
        right_side = (position >= width).astype(jnp.int32)
        group = 2 * group + right_side
        slot = position - width * right_side
    local = look_up(jnp.broadcast_to(leaf_ref[...], (width, width)))
    return jnp.where(group == own_row, local, -1)


def step_kernel(
    row_devices,
    col_devices,
    panel_hbm,
    trailing_hbm,
    prev_hbm,
    prev_upper_hbm,
    leaf_hbm,
    merge_hbm,
    lower_hbm,
    u_hbm,
    right_hbm,
    updated_hbm,
    gram_hbm,
    trailing_ref,
    prev_upper_ref,
    leaf_ref,
    merge_ref,
    lower_ref,
    u_ref,
    right_ref,
    gram_ref,
    tall,
    picked,
    picked_in,
    block,
    trail,
    trail_in,
    trail_all,
    w,
    x,
    linv,
    uinvt,
    lower_full,
    gram_in,
    tall_send,
    tall_recv,
    row_send,
    row_recv,
    zone_send,
    zone_recv,
    own_sem,
    in_sem,
    piece_sem,
    out_sem,
):
    slab, rows_here = panel_hbm.shape
    order = merge_ref.shape[1]
    trail_cols = trailing_ref.shape[1]
    share = order // row_devices
    span = rows_here // HALF
    own_row = lax.axis_index("rows")
    own_col = lax.axis_index("cols")

    barrier = pltpu.get_barrier_semaphore()

    @pl.loop(1, row_devices)
    def _(d):
        pl.semaphore_signal(
            barrier,
            inc=1,
            device_id={"rows": lax.rem(own_row + d, row_devices)},
            device_id_type=MESH,
        )

    @pl.loop(1, col_devices)
    def _(d):
        pl.semaphore_signal(
            barrier,
            inc=1,
            device_id={"cols": lax.rem(own_col + d, col_devices)},
            device_id_type=MESH,
        )

    own_copies = []
    for q in range(PIECES):
        source = panel_hbm if q < HALF else prev_hbm
        part = pl.ds(q % HALF * span, span)
        own_copies.append(
            pltpu.make_async_copy(source.at[:, part], tall.at[q, own_col], own_sem.at[q])
        )
    loads = [
        pltpu.make_async_copy(source, place, in_sem.at[i])
        for i, (source, place) in enumerate(
            (
                (merge_hbm, merge_ref),
                (leaf_hbm, leaf_ref),
                (trailing_hbm, trailing_ref),
                (prev_upper_hbm, prev_upper_ref),
            )
        )
    ]
    for copy in loads[:2] + own_copies + loads[2:]:
        copy.start()
    pl.semaphore_wait(barrier, row_devices + col_devices - 2)

    def tall_copy(q, source, way, to):
        place = tall.at[q, source]
        return pltpu.make_async_remote_copy(
            src_ref=place,
            dst_ref=place,
            send_sem=tall_send.at[way, source, q],
            recv_sem=tall_recv.at[source, q],
            device_id={"cols": to},
            device_id_type=MESH,
        )

    def step_up(hop, q):
        up = own_col - hop
        if hop > 0:

            @pl.when(up >= 0)
            def _():
                tall_copy(q, up, 0, own_col - 1).wait_recv()

        @pl.when((up >= 0) & (own_col < col_devices - 1))
        def _():
            tall_copy(q, up, 0, own_col + 1).start()

    def step_down(hop, q):
        down = own_col + hop
        if hop > 0:

            @pl.when(down < col_devices)
            def _():
                tall_copy(q, down, 1, own_col + 1).wait_recv()

        @pl.when((down < col_devices) & (own_col > 0))
        def _():
            tall_copy(q, down, 1, own_col - 1).start()

    def step(hop, q):
        @pl.when(own_col < col_devices // 2)
        def _():
            step_down(hop, q)
            step_up(hop, q)

        @pl.when(own_col >= col_devices // 2)
        def _():
            step_up(hop, q)
            step_down(hop, q)

    def share_of(d):
        return pl.ds(pl.multiple_of(lax.rem(own_row + d, row_devices) * share, share), share)

    def row_copy(kind, d, src, dst):
        return pltpu.make_async_remote_copy(
            src_ref=src,
            dst_ref=dst,
            send_sem=row_send.at[kind, d],
            recv_sem=row_recv.at[kind, d],
            device_id={"rows": lax.rem(own_row + d, row_devices)},
            device_id_type=MESH,
        )

    def picked_copy(d):
        return row_copy(0, d, picked.at[share_of(d), :], picked_in.at[d])

    def block_copy(d):
        return row_copy(1, d, block.at[own_row], block.at[own_row])

    def trail_copy(d):
        return row_copy(2, d, trail.at[share_of(d), :], trail_in.at[d])

    def trail_out_copy(d):
        return row_copy(3, d, trail_all.at[own_row], trail_all.at[own_row])

    def gram_copy(d):
        return row_copy(4, d, gram_in.at[0], gram_in.at[d])

    def zone_copy(d):
        return pltpu.make_async_remote_copy(
            src_ref=block.at[own_row, own_col],
            dst_ref=block.at[own_row, own_col],
            send_sem=zone_send.at[d],
            recv_sem=zone_recv.at[d],
            device_id={"cols": lax.rem(own_col + d, col_devices)},
            device_id_type=MESH,
        )

    def start_all(copy, count):
        @pl.loop(1, count)
        def _(d):
            copy(d).start()

    def land_all(copy, count):
        @pl.loop(1, count)
        def _(d):
            copy(d).wait_recv()

    def sent_all(copy, count):
        @pl.loop(1, count)
        def _(d):
            copy(d).wait_send()

    for q in range(HALF):
        own_copies[q].wait()
        step(0, q)
    for copy in own_copies[HALF:]:
        copy.wait()
    loads[0].wait()
    loads[1].wait()
    target = trace_rows(merge_ref, leaf_ref, row_devices, own_row)
    lane = lax.broadcasted_iota(jnp.int32, (order, span), 1)

    def one_hot(q):
        return jnp.where(lane + q * span == target, 1.0, 0.0).astype(jnp.bfloat16)

    total = jnp.zeros((order, 128), jnp.float32)
    for q in range(HALF):
        stack = jnp.concatenate([tall[q, own_col], tall[q + HALF, own_col]], 0)
        if 2 * slab < 128:
            stack = jnp.concatenate([stack, jnp.zeros((128 - 2 * slab, span), jnp.float32)], 0)
        found = lax.dot_general(
            one_hot(q),
            jnp.concatenate(pieces(stack), 0),
            (((1,), (1,)), ((), ())),
            preferred_element_type=jnp.float32,
        )
        total = total + (found[:, :128] + found[:, 128:256] + found[:, 256:])
    picked[...] = total
    start_all(picked_copy, row_devices)
    loads[2].wait()
    loads[3].wait()

    total = jnp.zeros((order, trail_cols), jnp.float32)
    for q in range(HALF):
        chosen = one_hot(q)
        for part in pieces(trailing_ref[q * span : (q + 1) * span, :]):
            total = total + jnp.dot(chosen, part, preferred_element_type=jnp.float32)
    trail[...] = total

    land_all(picked_copy, row_devices)
    total = picked[share_of(0), :]
    for d in range(1, row_devices):
        total = total + picked_in[d]
    block[own_row, own_col] = total
    start_all(zone_copy, col_devices)
    for q in range(HALF, HALF + 2):
        step(0, q)
    land_all(zone_copy, col_devices)
    start_all(block_copy, row_devices)
    start_all(trail_copy, row_devices)
    for q in range(HALF + 2, PIECES):
        step(0, q)
    land_all(block_copy, row_devices)

    def gathered(first):
        parts = []
        for z in range(col_devices):
            parts.append(block[:, z].reshape(order, 128)[:, first : first + slab])
        return jnp.concatenate(parts, 1)

    matrix = gathered(0)
    w[...] = matrix
    x[...] = matrix.T

    count = order // BLOCK
    early = PIECES // (count // 2)

    @pl.loop(0, count)
    def _(stage):
        lu_stage(stage, order, w, x, u_ref, linv, uinvt)

        @pl.when(stage < count // 2)
        def _():
            for part in range(early):
                step(1, stage * early + part)

        @pl.when(stage >= count // 2)
        def _():
            step(2, stage - count // 2)

        @pl.when(stage == 2)
        def _():
            land_all(trail_copy, row_devices)
            total = trail[share_of(0), :]
            for d in range(1, row_devices):
                total = total + trail_in[d]
            trail_all[own_row] = total
            start_all(trail_out_copy, row_devices)

    land_all(trail_out_copy, row_devices)
    chosen = trail_all[...].reshape(order, trail_cols)
    chosen = chosen - product(gathered(slab), prev_upper_ref[...])
    right_ref[...] = product(linv[...], chosen)
    gram_in[0] = jnp.zeros((slab, order), jnp.float32)
    u_copy = pltpu.make_async_copy(u_ref, u_hbm, out_sem.at[0])
    right_copy = pltpu.make_async_copy(right_ref, right_hbm, out_sem.at[1])
    u_copy.start()
    right_copy.start()
    for hop in range(2, col_devices - 1):

        @pl.loop(count // 2 if hop == 2 else 0, PIECES)
        def _(q):
            step(hop, q)

    def piece_copies(q):
        here = pl.ds(pl.multiple_of(q * span, span), span)
        return (
            pltpu.make_async_copy(lower_ref.at[:, here], lower_hbm.at[:, here], piece_sem.at[0, q]),
            pltpu.make_async_copy(
                trailing_ref.at[here, :], updated_hbm.at[here, :], piece_sem.at[1, q]
            ),
        )

    @pl.loop(0, HALF)
    def _(q):
        step(col_devices - 1, q)
        here = pl.ds(pl.multiple_of(q * span, span), span)
        lower = product(uinvt[...], tall[q].reshape(order, span))
        lower_full[q] = lower
        tile = lower_full[q, pl.ds(pl.multiple_of(own_col * slab, slab), slab), :]
        lower_ref[:, here] = tile
        piece_copies(q)[0].start()
        gram_in[0] += product(tile, lower, 1, 1)

        @pl.when(q == HALF - 1)
        def _():
            start_all(gram_copy, row_devices)

        trailing_ref[here, :] = trailing_ref[here, :] - product(lower, right_ref[...], 0, 0)

    def last_copy():
        return pltpu.make_async_copy(gram_ref, gram_hbm, out_sem.at[2])

    @pl.loop(0, HALF)
    def _(q):
        @pl.when(q == HALF - 1)
        def _():
            land_all(gram_copy, row_devices)
            total = gram_in[0]
            for d in range(1, row_devices):
                total = total + gram_in[d]
            gram_ref[...] = total / (rows_here * row_devices)
            last_copy().start()

        step(col_devices - 1, q + HALF)
        here = pl.ds(pl.multiple_of(q * span, span), span)
        prev_full = tall[q + HALF].reshape(order, span)
        trailing_ref[here, :] = trailing_ref[here, :] - product(
            prev_full, prev_upper_ref[...], 0, 0
        )
        piece_copies(q)[1].start()

    sent_all(picked_copy, row_devices)
    sent_all(zone_copy, col_devices)
    sent_all(block_copy, row_devices)
    sent_all(trail_copy, row_devices)
    sent_all(trail_out_copy, row_devices)

    @pl.loop(0, PIECES)
    def _(q):
        @pl.loop(0, col_devices)
        def _(source):
            @pl.when((source <= own_col) & (own_col < col_devices - 1))
            def _():
                tall_copy(q, source, 0, own_col + 1).wait_send()

            @pl.when((source >= own_col) & (own_col > 0))
            def _():
                tall_copy(q, source, 1, own_col - 1).wait_send()

    sent_all(gram_copy, row_devices)

    @pl.loop(0, HALF)
    def _(q):
        for copy in piece_copies(q):
            copy.wait()

    u_copy.wait()
    right_copy.wait()
    last_copy().wait()


def place_kernel(*refs):
    sources, places, held, in_sem, out_sem = refs[:5], refs[5:10], refs[10:15], refs[15], refs[16]
    arrivals, departures = [], []
    for source, place, middle in zip(sources, places, held):
        height = source.shape[0]
        parts = 4 if height >= 1024 else 1
        for part in range(parts):
            rows = pl.ds(part * (height // parts), height // parts)
            here = middle.at[rows, :]
            index = len(arrivals)
            arrivals.append(pltpu.make_async_copy(source.at[rows, :], here, in_sem.at[index]))
            departures.append(pltpu.make_async_copy(here, place.at[rows, :], out_sem.at[index]))
    for copy in arrivals:
        copy.start()
    for arrival, departure in zip(arrivals, departures):
        arrival.wait()
        departure.start()
    for copy in departures:
        copy.wait()


def body(row_devices, col_devices, panel_t, trailing, prev_lower_t, prev_upper, leaf, merge):
    slab, rows_here = panel_t.shape
    order = merge.shape[1]
    trail_cols = trailing.shape[1]
    share = order // row_devices
    span = rows_here // HALF
    real = jnp.float32
    square = pltpu.VMEM((order, order), real)
    anywhere = pl.BlockSpec(memory_space=pl.ANY)
    dma = pltpu.SemaphoreType.DMA
    shapes = [
        jax.ShapeDtypeStruct((slab, rows_here), real),
        jax.ShapeDtypeStruct((order, order), real),
        jax.ShapeDtypeStruct((order, trail_cols), real),
        jax.ShapeDtypeStruct((rows_here, trail_cols), real),
        jax.ShapeDtypeStruct((slab, order), real),
    ]
    results = pl.pallas_call(
        functools.partial(step_kernel, row_devices, col_devices),
        out_shape=shapes,
        in_specs=[anywhere] * 6,
        out_specs=[anywhere] * 5,
        scratch_shapes=[
            pltpu.VMEM((rows_here, trail_cols), real),
            pltpu.VMEM((order, trail_cols), real),
            pltpu.VMEM((1, order), jnp.int32),
            pltpu.VMEM(merge.shape, jnp.int32),
            pltpu.VMEM((slab, rows_here), real),
            square,
            pltpu.VMEM((order, trail_cols), real),
            pltpu.VMEM((slab, order), real),
            pltpu.VMEM((PIECES, col_devices, slab, span), real),
            pltpu.VMEM((order, 128), real),
            pltpu.VMEM((row_devices, share, 128), real),
            pltpu.VMEM((row_devices, col_devices, share, 128), real),
            pltpu.VMEM((order, trail_cols), real),
            pltpu.VMEM((row_devices, share, trail_cols), real),
            pltpu.VMEM((row_devices, share, trail_cols), real),
            square,
            square,
            square,
            square,
            pltpu.VMEM((HALF, order, span), real),
            pltpu.VMEM((row_devices, slab, order), real),
            dma((2, col_devices, PIECES)),
            dma((col_devices, PIECES)),
            dma((5, row_devices)),
            dma((5, row_devices)),
            dma((col_devices,)),
            dma((col_devices,)),
            dma((PIECES,)),
            dma((4,)),
            dma((2, HALF)),
            dma((3,)),
        ],
        compiler_params=pltpu.CompilerParams(
            collective_id=0, has_side_effects=True, vmem_limit_bytes=56 * 1024 * 1024
        ),
        name="panel_step",
    )(panel_t, trailing, prev_lower_t, prev_upper, leaf, merge)
    return pl.pallas_call(
        place_kernel,
        out_shape=shapes,
        in_specs=[anywhere] * 5,
        out_specs=[anywhere] * 5,
        scratch_shapes=[pltpu.VMEM(shape.shape, real) for shape in shapes] + [dma((8,))] * 2,
        compiler_params=pltpu.CompilerParams(vmem_limit_bytes=56 * 1024 * 1024),
        name="place_outputs",
    )(*results)


def solution(mesh):
    return jax.shard_map(
        functools.partial(body, mesh.shape["rows"], mesh.shape["cols"]),
        mesh=mesh,
        in_specs=(
            P("cols", "rows"),
            P("rows", "cols"),
            P("cols", "rows"),
            P(None, "cols"),
            P("rows", None),
            P(),
        ),
        out_specs=(P("cols", "rows"), P(), P(None, "cols"), P("rows", "cols"), P("cols", None)),
        check_vma=False,
    )
```
